128 devices in a mesh: dp: 8 (over y, core), tensor: 16 (over x, z).
Axes of the slice: x: 4, y: 4, z: 4, core: 2. Of those that a mesh axis runs over, the one named last changes fastest.
Arguments:
- activations: bfloat16 [8192, 5120], P('dp', 'tensor'), may hold values from -6 to 6
- upstream: bfloat16 [8192, 5120], P('dp', 'tensor'), may hold values from -6 to 6
- gate_pre: bfloat16 [8192, 27648], P('dp', 'tensor'), may hold values from -8 to 8
- up_out: bfloat16 [8192, 27648], P('dp', 'tensor'), may hold values from -6 to 6
- w_down: bfloat16 [27648, 5120], P('tensor'), may hold values from -0.078125 to 0.078125
- proj_in: bfloat16 [64, 5120], P(None, 'tensor'), may hold values from -0.078125 to 0.078125
- proj_out: bfloat16 [64, 27648], P(None, 'tensor'), may hold values from -0.0390625 to 0.0390625
- policy_logp: float32 [32, 256], P('dp', 'tensor'), may hold values from -4 to 0
- ref_logp: float32 [32, 256], P('dp', 'tensor'), may hold values from -4 to 0
- loss_mask: int32 [32, 256], P('dp'), may hold values 0 or 1
- resp_len: int32 [32], P('dp'), may hold values from 32 to 256, as said below
- pair_perm: int32 [8, 4], P('dp'), may hold values from 0 to 3, each once within a row
- chosen_first: int32 [16], P('dp'), may hold values 0 or 1
Outputs:
- pair_grads: float32 [16, 4096], P('dp')
- fisher: float32 [4096, 4096], P('tensor', 'dp')
The draws below stay inside these ranges and needn't reach their ends.
Inputs may be any that keep to these rules, and one draw needn't show every extreme that they name: `resp_len`: at least 32; every index of dp holds a sequence with the full 256 response tokens.
All inputs are finite; a program needn't handle non-finite values. No bound on the sum of `loss_mask` or of `chosen_first` on one device may be relied on, other than what follows from the above.
Results may differ from the reference program's by a relative error of at most 0.0041.
Values may be sent and summed in bfloat16 or wider, within the bound.
A program may use at most 128 MiB of HBM per device.

```python
import jax
import jax.numpy as jnp
from jax import lax

D = 5120
FF = 27648
R = 64
LEN = 256
SEQS_DEV = 4
PROJ = 4096
GROUPS = 8
PAIRS = 16
SEQS = 32
TOKENS = 8192


def draw_resp_len(key, part):
    key = jax.random.fold_in(key, 7)
    values = jax.random.randint(key, (SEQS,), LEN // 8, LEN + 1, dtype=jnp.int32)
    offsets = jax.random.randint(jax.random.fold_in(key, 11), (GROUPS,), 0, SEQS_DEV, dtype=jnp.int32)
    slots = jnp.arange(GROUPS, dtype=jnp.int32) * SEQS_DEV + offsets
    return values.at[slots].set(LEN)


def touch_ends(array, stream_key, low, top_value):
    index_at = [jax.random.randint(jax.random.fold_in(stream_key, axis), (), 0, length) for axis, length in enumerate(array.shape)]
    widest = array.shape.index(max(array.shape))
    beside = index_at[:widest] + [(index_at[widest] + 1) % array.shape[widest]] + index_at[widest + 1:]
    return array.at[tuple(index_at)].set(low).at[tuple(beside)].set(top_value)


def steps_of(own_key, shape, pieces, low, high):
    level, own = 1.0, jax.random.fold_in(own_key, 6)
    for axis_at, parts in pieces:
        draws = jnp.exp(jax.random.uniform(jax.random.fold_in(own, axis_at), (parts,), jnp.float32, low / len(pieces), high / len(pieces)))
        level = level * jnp.repeat(draws, shape[axis_at] // parts).reshape([-1 if axis == axis_at else 1 for axis in range(len(shape))])
    return level


def noise(own_key, dims, deviation, most, pieces=(), held_as=jnp.bfloat16):
    array = deviation * jax.random.normal(own_key, dims, jnp.float32)
    if pieces:
        array = array * steps_of(own_key, dims, pieces, -0.22, 0.18)
    return jnp.clip(array, -most, most).astype(held_as)


def setup_inputs(seed: int = 0) -> dict:
    keys = jax.random.split(jax.random.key(seed), 14)
    activations = noise(keys[0], (TOKENS, D), 1.0, 6.0, ((0, 8), (1, 16)))
    upstream = noise(keys[1], (TOKENS, D), 1.0, 6.0, ((0, 8), (1, 16)))
    gate_pre = noise(keys[2], (TOKENS, FF), 2.0, 8.0, ((0, 8), (1, 16)))
    up_out = noise(keys[3], (TOKENS, FF), 1.0, 6.0, ((0, 8), (1, 16)))
    w_down = noise(keys[4], (FF, D), D ** -0.5, 0.078125, ((0, 16),))
    proj_in = noise(keys[5], (R, D), D ** -0.5, 0.078125, ((1, 16),))
    proj_out = noise(keys[6], (R, FF), FF ** -0.5, 0.0390625, ((1, 16),))
    policy_logp = jnp.clip(-4.0 + 4.0 * jax.random.uniform(keys[7], (SEQS, LEN), jnp.float32) ** steps_of(keys[7], (SEQS, LEN), ((0, 8), (1, 16)), -0.2, 0.2), -4.0, 0.0)
    ref_logp = jnp.clip(-4.0 + 4.0 * jax.random.uniform(keys[8], (SEQS, LEN), jnp.float32) ** steps_of(keys[8], (SEQS, LEN), ((0, 8), (1, 16)), -0.2, 0.2), -4.0, 0.0)
    loss_mask = touch_ends((jax.random.randint(keys[9], (SEQS, LEN), 0, 4) < 3).astype(jnp.int32), jax.random.fold_in(keys[9], 1), 0, 1)
    resp_len = draw_resp_len(jax.random.fold_in(keys[13], 71), 0)
    pair_perm = jax.vmap(lambda own: jax.random.permutation(own, SEQS_DEV))(jax.random.split(keys[11], GROUPS)).reshape((GROUPS, SEQS_DEV)).astype(jnp.int32)
    chosen_first = touch_ends((jax.random.randint(keys[12], (PAIRS,), 0, 2) < 1).astype(jnp.int32), jax.random.fold_in(keys[12], 1), 0, 1)
    return dict(activations=activations, upstream=upstream, gate_pre=gate_pre, up_out=up_out, w_down=w_down, proj_in=proj_in, proj_out=proj_out, policy_logp=policy_logp, ref_logp=ref_logp, loss_mask=loss_mask, resp_len=resp_len, pair_perm=pair_perm, chosen_first=chosen_first)


BETA = 0.1


def reference(activations, upstream, gate_pre, up_out, w_down, proj_in, proj_out, policy_logp, ref_logp, loss_mask, resp_len, pair_perm, chosen_first):
    positions = jnp.arange(LEN, dtype=jnp.int32)
    live = (positions[None, :] >= (LEN - resp_len)[:, None]) & (loss_mask == 1)
    weight = live.astype(jnp.float32)
    margin = jnp.sum(weight * (policy_logp - ref_logp), axis=1)
    x_all = activations.reshape(SEQS, LEN, D)
    dy_all = upstream.reshape(SEQS, LEN, D)
    g_all = gate_pre.reshape(SEQS, LEN, FF)
    u_all = up_out.reshape(SEQS, LEN, FF)

    def one_sequence(item):
        x_seq, dy_seq, g_seq, u_seq, w_seq = item
        hidden_grad = jnp.dot(dy_seq, w_down.T, preferred_element_type=jnp.float32)
        gate = g_seq.astype(jnp.float32)
        sigma_gate = jax.nn.sigmoid(gate)
        gate_grad = (hidden_grad * u_seq.astype(jnp.float32) * sigma_gate * (1.0 + gate * (1.0 - sigma_gate))).astype(jnp.bfloat16)
        out_side = jnp.dot(gate_grad, proj_out.T, preferred_element_type=jnp.float32)
        in_side = jnp.dot(x_seq, proj_in.T, preferred_element_type=jnp.float32)
        return jnp.dot((in_side * w_seq[:, None]).T, out_side, precision=lax.Precision.HIGHEST).reshape(PROJ)

    blocks = lax.map(one_sequence, (x_all, dy_all, g_all, u_all, weight))
    base = (jnp.arange(GROUPS, dtype=jnp.int32) * SEQS_DEV)[:, None]
    first = (pair_perm[:, 0::2] + base).reshape(PAIRS)
    second = (pair_perm[:, 1::2] + base).reshape(PAIRS)
    chosen = chosen_first == 1
    chosen_seq = jnp.where(chosen, first, second)
    rejected_seq = jnp.where(chosen, second, first)
    coeff = -BETA * jax.nn.sigmoid(-BETA * (margin[chosen_seq] - margin[rejected_seq]))
    pair_grads = coeff[:, None] * (blocks[chosen_seq] - blocks[rejected_seq])
    fisher = jnp.dot(pair_grads.T, pair_grads, precision=lax.Precision.HIGHEST)
    return pair_grads, fisher
```

```python
import functools

import jax
import jax.numpy as jnp
from jax import lax
from jax.experimental import pallas as pl
from jax.experimental.pallas import tpu as pltpu
from jax.sharding import PartitionSpec as P

BETA = 0.1
F32, BF16, I32 = jnp.float32, jnp.bfloat16, jnp.int32
MESH = pl.DeviceIdType.MESH
NT = (((1,), (1,)), ((), ()))
TN = (((0,), (0,)), ((), ()))

TENSOR = 16
GROUPS = 8
SEQS = 4
LEN = 256
TOKENS = SEQS * LEN
RANK = 64
FEATURES = 320
HIDDEN = 1728
MODEL = TENSOR * FEATURES
CHUNK = 64
ROWS = 160
HALF = 80
PAIR = 2 * CHUNK
ALL_PAIRS = TOKENS // PAIR
PRE = 4


def iota(shape, axis):
    return lax.broadcasted_iota(I32, shape, axis)


def place():
    g, t = lax.axis_index("dp"), lax.axis_index("tensor")
    return g, t, t // 4, t % 4


def stepped(v, by):
    return lax.rem(v + by + 4, 4)


def remote(src, dst, send, recv, g, t):
    return pltpu.make_async_remote_copy(
        src_ref=src, dst_ref=dst, send_sem=send, recv_sem=recv, device_id={"dp": g, "tensor": t}, device_id_type=MESH
    )


def neighbour(axis, by, x, z):
    return stepped(x, by) * 4 + z if axis == 0 else x * 4 + stepped(z, by)


def pair_sign(perm, first, pair, seq):
    side = jnp.where(first[pair] == 1, 1.0, -1.0).astype(F32)
    is_a = jnp.where(perm[0, 2 * pair] == seq, 1.0, 0.0).astype(F32)
    is_b = jnp.where(perm[0, 2 * pair + 1] == seq, 1.0, 0.0).astype(F32)
    return side * (is_a - is_b)


def stage_kernel(
    perm, first, resp, mask, pol, ref, up, act, pin,
    own_o, g1_o, pick_o, sign_o, insum_o, count_o, gap_o,
    pick, cols, own, packed, part, parts, counts, mine,
    keep, ssend, srecv, isend, irecv, csend, crecv,
):
    g, t, x, z = place()
    barrier = pltpu.get_barrier_semaphore()
    for d in range(1, TENSOR):
        pl.semaphore_signal(barrier, inc=1, device_id={"dp": g, "tensor": lax.rem(t + d, TENSOR)}, device_id_type=MESH)
    for d in range(1, GROUPS):
        pl.semaphore_signal(barrier, inc=1, device_id={"dp": lax.rem(g + d, GROUPS), "tensor": t}, device_id_type=MESH)

    row4 = iota((SEQS, LEN), 0)
    start = jnp.zeros((SEQS, LEN), I32)
    for s in range(SEQS):
        start = jnp.where(row4 == s, LEN - resp[s], start)
    live = (iota((SEQS, LEN), 1) >= start) & (mask[...] == 1)
    live_f = jnp.where(live, 1.0, 0.0).astype(F32)
    upto = jnp.where(iota((LEN, LEN), 0) <= iota((LEN, LEN), 1), 1.0, 0.0).astype(BF16)
    running = jnp.dot(live_f.astype(BF16), upto, preferred_element_type=F32)
    begins = [jnp.zeros((1, 1), F32)]
    for s in range(SEQS):
        begins.append(begins[s] + running[s : s + 1, LEN - 1 : LEN])
    for s in range(SEQS):
        at = jnp.where(live[s : s + 1, :], running[s : s + 1, :] - 1.0 + begins[s], -1.0).astype(I32)
        pick[:, s * LEN : (s + 1) * LEN] = jnp.where(iota((TOKENS, LEN), 0) == at, 1.0, 0.0).astype(BF16)
    mine[...] = jnp.broadcast_to(begins[SEQS], (8, 128))

    odd = lax.rem(t, 2)
    r, c = iota((512, FEATURES), 1), iota((512, FEATURES), 0)
    wide = (c < 256) & (r == c + 64 * odd)
    base = jnp.where(odd == 1, 0, 256)
    low = (c >= 256) & (c < 384) & (c - 256 - 64 * odd >= 0) & (c - 256 - 64 * odd < 64) & (r == base + c - 256 - 64 * odd)
    other = 64 * (1 - odd)
    high = (c >= 384) & (c - 384 - other >= 0) & (c - 384 - other < 64) & (r == base + c - 384 - other)
    order = jnp.where(wide | low | high, 1.0, 0.0).astype(BF16)
    cols[...] = jnp.dot(order, up[...], preferred_element_type=F32).astype(BF16)

    def fill(q):
        rows = pl.ds(pl.multiple_of(q * PAIR, PAIR), PAIR)
        moved = lax.dot_general(pick[rows, :], cols[...], NT, preferred_element_type=F32)
        for par in range(2):
            lo = par * CHUNK
            own[par, q, 0:64, :] = moved[lo : lo + 64, 0:128].astype(BF16)
            own[par, q, 64:128, :] = moved[lo : lo + 64, 128:256].astype(BF16)
            own[par, q, 128:160, :] = (moved[lo : lo + 32, 256:384] + moved[lo + 32 : lo + 64, 384:512]).astype(BF16)

    pl.loop(0, PRE)(fill)
    pl.semaphore_wait(barrier, TENSOR - 1 + GROUPS - 1)

    hop1, hop2 = [], []
    for par in range(2):
        slot = x if par == 0 else z
        for k, by in enumerate((1, -1)):
            i = par * 2 + k
            to = neighbour(par, by, x, z)
            hop1.append(remote(own.at[par, 0:PRE], g1_o.at[par, :, slot], ssend.at[i], srecv.at[i], g, to))
            held = g1_o.at[par, :, stepped(slot, -by), k * HALF : (k + 1) * HALF]
            hop2.append(remote(held, held, ssend.at[4 + i], srecv.at[4 + i], g, to))
    for cp in hop1:
        cp.start()
    tells = []
    for d in range(1, GROUPS):
        cp = remote(mine, counts.at[g], csend.at[d - 1], crecv.at[d - 1], lax.rem(g + d, GROUPS), t)
        cp.start()
        tells.append(cp)

    pl.loop(PRE, ALL_PAIRS)(fill)
    keeps = [pltpu.make_async_copy(own, own_o, keep.at[0]), pltpu.make_async_copy(pick, pick_o, keep.at[3])]
    for par in range(2):
        slot = x if par == 0 else z
        keeps.append(pltpu.make_async_copy(own.at[par, 0:PRE], g1_o.at[par, :, slot], keep.at[1 + par]))
    for cp in keeps:
        cp.start()

    packed[...] = lax.dot_general(pick[...], act[...], NT, preferred_element_type=F32).astype(BF16)
    none = jnp.zeros((RANK, FEATURES), BF16)
    sides = lax.dot_general(packed[0:512, :], jnp.concatenate([pin[...], none], 0), NT, preferred_element_type=F32)
    sides += lax.dot_general(packed[512:1024, :], jnp.concatenate([none, pin[...]], 0), NT, preferred_element_type=F32)
    part[...] = sides.reshape(TENSOR, 32, 128)
    halves = []
    for d in range(1, TENSOR):
        to = lax.rem(t + d, TENSOR)
        cp = remote(part.at[to], parts.at[t], isend.at[d - 1], irecv.at[d - 1], g, to)
        cp.start()
        halves.append(cp)

    for cp in hop1:
        cp.wait_recv()
    for cp in hop2:
        cp.start()

    k_at = iota((TOKENS, 128), 0)
    pair_at = lax.rem(iota((TOKENS, 128), 1) // 4, 2)
    sign = jnp.zeros((TOKENS, 128), F32)
    for s in range(SEQS):
        inside = (k_at >= begins[s].astype(I32)) & (k_at < begins[s + 1].astype(I32))
        value = jnp.where(pair_at == 0, pair_sign(perm, first, 0, s), pair_sign(perm, first, 1, s))
        sign = jnp.where(inside, value, sign)
    sign_o[...] = sign.astype(BF16)

    span = jnp.where(iota((LEN, 16), 0) == t * 16 + iota((LEN, 16), 1), 1.0, 0.0).astype(BF16)
    weights = jnp.dot(live_f.astype(BF16), span, preferred_element_type=F32)
    margin = jnp.sum(weights * (pol[...] - ref[...]), axis=1, keepdims=True)
    gaps = []
    for p in range(2):
        gap = jnp.zeros((1, 1), F32)
        for s in range(SEQS):
            gap += pair_sign(perm, first, p, s) * margin[s : s + 1, :]
        gaps.append(gap)
    gap_o[...] = jnp.where(iota((8, 128), 0) < 4, gaps[0], gaps[1])

    for cp in halves:
        cp.wait_recv()
    parts[t] = part[t]
    total = parts[0]
    for i in range(1, TENSOR):
        total += parts[i]
    insum_o[...] = total.astype(BF16)
    for cp in tells:
        cp.wait_recv()
    counts[g] = mine[...]
    most = counts[0]
    for i in range(1, GROUPS):
        most = jnp.maximum(most, counts[i])
    count_o[...] = most.astype(I32)
    for cp in hop2:
        cp.wait_recv()
    for cp in hop1 + hop2 + halves + tells:
        cp.wait_send()
    for cp in keeps:
        cp.wait()


def stage(perm, first, resp, mask, pol, ref, up, act, pin):
    sds = jax.ShapeDtypeStruct
    vmem = pl.BlockSpec(memory_space=pltpu.VMEM)
    smem = pl.BlockSpec(memory_space=pltpu.SMEM)
    hbm = pl.BlockSpec(memory_space=pl.ANY)
    dma = pltpu.SemaphoreType.DMA
    return pl.pallas_call(
        stage_kernel,
        out_shape=(
            sds((2, ALL_PAIRS, ROWS, 128), BF16),
            sds((2, PRE, 4, ROWS, 128), BF16),
            sds((TOKENS, TOKENS), BF16),
            sds((TOKENS, 128), BF16),
            sds((32, 128), BF16),
            sds((8, 128), I32),
            sds((8, 128), F32),
        ),
        in_specs=[smem] * 3 + [vmem] * 6,
        out_specs=(hbm, hbm, hbm, vmem, vmem, vmem, vmem),
        scratch_shapes=[
            pltpu.VMEM((TOKENS, TOKENS), BF16),
            pltpu.VMEM((512, TOKENS), BF16),
            pltpu.VMEM((2, ALL_PAIRS, ROWS, 128), BF16),
            pltpu.VMEM((TOKENS, FEATURES), BF16),
            pltpu.VMEM((TENSOR, 32, 128), F32),
            pltpu.VMEM((TENSOR, 32, 128), F32),
            pltpu.VMEM((GROUPS, 8, 128), F32),
            pltpu.VMEM((8, 128), F32),
            dma((4,)),
            dma((8,)),
            dma((8,)),
            dma((TENSOR - 1,)),
            dma((TENSOR - 1,)),
            dma((GROUPS - 1,)),
            dma((GROUPS - 1,)),
        ],
        compiler_params=pltpu.CompilerParams(collective_id=0, has_side_effects=True, vmem_limit_bytes=56 << 20),
        cost_estimate=pl.CostEstimate(flops=2_000_000_000, bytes_accessed=8_000_000, transcendentals=0),
        name="stage",
    )(perm, first, resp, mask, pol, ref, up, act, pin)


def main_kernel(
    pairs, sign, insum, gap, pout, own_h, g1_h, pick_h, gate_h, upo_h, w_h,
    ends_o,
    blocks, w, gate, upo, pick, m, u, grad, sides, diff, outs, ins, fin, every, rowed, coled,
    load, asend, arecv, fsend, frecv, ssend, srecv, rsend, rrecv, gsend, grecv, psend, precv, csend, crecv,
):
    g, t, x, z = place()
    column_group, column_part = t // 2, lax.rem(t, 2)
    barrier = pltpu.get_barrier_semaphore()
    for d in range(1, TENSOR):
        pl.semaphore_signal(barrier, inc=1, device_id={"dp": g, "tensor": lax.rem(t + d, TENSOR)}, device_id_type=MESH)
    for d in range(1, GROUPS):
        pl.semaphore_signal(barrier, inc=1, device_id={"dp": lax.rem(g + d, GROUPS), "tensor": t}, device_id_type=MESH)
    for d in range(GROUPS):
        for h in range(2):
            of, at = lax.rem(g + d, GROUPS), 2 * g + h

            def greet(of=of, at=at):
                pl.semaphore_signal(barrier, inc=1, device_id={"dp": of, "tensor": at}, device_id_type=MESH)

            if d == 0:
                pl.when(at != t)(greet)
            else:
                greet()

    wide = MODEL // 4
    loads = []
    halves = [
        pltpu.make_async_copy(pick_h.at[0 : pairs * PAIR], pick, load.at[9]),
        pltpu.make_async_copy(gate_h, gate, load.at[0]),
        pltpu.make_async_copy(upo_h, upo, load.at[10]),
    ]
    for par in range(2):
        to = blocks.at[0, 0:PRE, :, z] if par == 0 else blocks.at[1, 0:PRE, x]
        loads.append(pltpu.make_async_copy(g1_h.at[par], to, load.at[1 + par]))
        if pairs > PRE:
            loads.append(pltpu.make_async_copy(own_h.at[par, PRE:pairs], blocks.at[par, PRE:pairs, x, z], load.at[3 + par]))
    w_loads = [pltpu.make_async_copy(w_h.at[:, i * wide : (i + 1) * wide], w.at[:, i * wide : (i + 1) * wide], load.at[5 + i]) for i in range(4)]
    for cp in loads + halves + w_loads:
        cp.start()
    mates = TENSOR - 1 + GROUPS - 1 + TENSOR
    pl.semaphore_wait(barrier, mates - jnp.where(column_group == g, 1, 0))
    for cp in loads:
        cp.wait()

    def second(q, i, hop):
        par, k = i // 2, i % 2
        by = 1 if k == 0 else -1
        if par == 0:
            to = neighbour(1, by, x, z)
            ref = blocks.at[0, q, :, z] if hop == 0 else blocks.at[0, q, :, stepped(z, -by), k * HALF : (k + 1) * HALF]
        else:
            to = neighbour(0, by, x, z)
            ref = blocks.at[1, q, x] if hop == 0 else blocks.at[1, q, stepped(x, -by), :, k * HALF : (k + 1) * HALF]
        return remote(ref, ref, ssend.at[q, hop * 4 + i], srecv.at[q, hop * 4 + i], g, to)

    def ahead(i, hop):
        par, k = i // 2, i % 2
        by = 1 if k == 0 else -1
        to = neighbour(par, by, x, z)
        if hop == 0:
            ref = blocks.at[par, PRE:pairs, x, z]
        elif par == 0:
            ref = blocks.at[0, PRE:pairs, stepped(x, -by), z, k * HALF : (k + 1) * HALF]
        else:
            ref = blocks.at[1, PRE:pairs, x, stepped(z, -by), k * HALF : (k + 1) * HALF]
        return remote(ref, ref, fsend.at[hop * 4 + i], frecv.at[hop * 4 + i], g, to)

    for q in range(2):
        for i in range(4):
            second(q, i, 0).start()
    if pairs > PRE:
        for i in range(4):
            ahead(i, 0).start()
    ins[t] = insum[...]
    gathers = []
    for d in range(1, TENSOR):
        cp = remote(insum, ins.at[t], asend.at[d - 1], arecv.at[d - 1], g, lax.rem(t + d, TENSOR))
        cp.start()
        gathers.append(cp)
    diff[...] = jnp.zeros_like(diff)
    for cp in halves:
        cp.wait()

    def factor(first_pair, count):
        rows = pl.ds(pl.multiple_of(first_pair * PAIR, PAIR), count * PAIR)

        @pl.loop(0, HIDDEN // 432)
        def _(i):
            units = pl.ds(pl.multiple_of(i * 432, 16), 432)
            v = lax.dot_general(gate[units, :], pick[rows, :], NT, preferred_element_type=F32)
            o = lax.dot_general(upo[units, :], pick[rows, :], NT, preferred_element_type=F32)
            sig = jax.nn.sigmoid(v)
            m[units, rows] = o * sig * (1.0 + v * (1.0 - sig))

    def compute(first_pair, count):
        tokens = count * PAIR
        lanes = iota((32, 128), 1) < 64
        for one in range(count):
            q = first_pair + one
            for par in range(2):
                for s in range(TENSOR // 2):
                    a, b = blocks.at[par, q, s // 2, 2 * (s % 2)], blocks.at[par, q, s // 2, 2 * (s % 2) + 1]
                    r, c = one * PAIR + par * CHUNK, s * 640
                    u[r : r + 64, c : c + 128] = a[0:64, :]
                    u[r : r + 64, c + 128 : c + 256] = a[64:128, :]
                    u[r : r + 64, c + 384 : c + 512] = b[0:64, :]
                    u[r : r + 64, c + 512 : c + 640] = b[64:128, :]
                    left, right = a[128:160, :].astype(F32), b[128:160, :].astype(F32)
                    u[r : r + 32, c + 256 : c + 384] = jnp.where(lanes, left, right).astype(BF16)
                    u[r + 32 : r + 64, c + 256 : c + 384] = pltpu.roll(jnp.where(lanes, right, left), 64, 1).astype(BF16)
        rows = pl.ds(pl.multiple_of(first_pair * PAIR, PAIR), tokens)

        @pl.loop(0, HIDDEN // 576)
        def _(i):
            units = pl.ds(pl.multiple_of(i * 576, 16), 576)
            acc = None
            for k in range(4):
                at = slice(k * wide, (k + 1) * wide)
                more = lax.dot_general(w[units, at], u[0:tokens, at], NT, preferred_element_type=F32)
                acc = more if acc is None else acc + more
            grad[units, 0:tokens] = (acc * m[units, rows]).astype(BF16)

        out_side = jnp.dot(pout[...], grad[:, 0:tokens], preferred_element_type=F32)
        r, c = iota((128, 128), 0), iota((128, 128), 1)
        for one in range(count):
            q = first_pair + one
            side_rows = pl.ds(pl.multiple_of(lax.rem(q, 4) * 4, 4), 4)
            spread = jnp.where(r == jnp.where(q >= 4, 64, 0) + (c // 8) * 4 + lax.rem(c, 4), 1.0, 0.0).astype(BF16)
            in_side = jnp.dot(ins[side_rows].reshape(PAIR, 128), spread, preferred_element_type=F32)
            signed = in_side * sign[pl.ds(pl.multiple_of(q * PAIR, PAIR), PAIR), :].astype(F32)
            part = out_side[:, one * PAIR : (one + 1) * PAIR]
            diff[...] += jnp.dot(part, signed, precision=lax.Precision.HIGHEST, preferred_element_type=F32)

    def turn(q):
        for i in range(4):
            second(q, i, 0).wait_recv()
        for i in range(4):
            second(q, i, 1).start()

    def send(q):
        for i in range(4):
            second(q, i, 0).start()

    full, rest = pairs // 2, pairs % 2
    factor(0, 2)

    @pl.loop(0, full + 1)
    def _(n):
        @pl.when(2 * n < pairs)
        def _():
            turn(2 * n)

        if pairs > PRE:

            @pl.when(n == 0)
            def _():
                for i in range(4):
                    ahead(i, 0).wait_recv()
                for i in range(4):
                    ahead(i, 1).start()

            @pl.when(n == 1)
            def _():
                for i in range(4):
                    ahead(i, 1).wait_recv()

        @pl.when(2 * n + 2 < pairs)
        def _():
            send(2 * n + 2)

        @pl.when(n + 1 < full)
        def _():
            factor(2 * n + 2, 2)

        if rest:

            @pl.when(n + 1 == full)
            def _():
                factor(2 * full, 1)

        @pl.when(2 * n + 1 < pairs)
        def _():
            turn(2 * n + 1)

        @pl.when(2 * n + 3 < pairs)
        def _():
            send(2 * n + 3)

        @pl.when(n == 1)
        def _():
            for cp in w_loads:
                cp.wait()
            for cp in gathers:
                cp.wait_recv()

        @pl.when(n >= 1)
        def _():
            for one in range(2):
                for i in range(4):
                    second(2 * n - 2 + one, i, 1).wait_recv()
            compute(2 * n - 2, 2)

    if rest:
        for i in range(4):
            second(pairs - 1, i, 1).wait_recv()
        compute(pairs - 1, 1)

    mine = jnp.concatenate([diff[...].T, jnp.broadcast_to(gap[0:1, 0:1], (128, 64))], 1).reshape(TENSOR, 8, 128)
    upper = (iota((TENSOR, 8, 128), 2) >= 64) & (iota((TENSOR, 8, 128), 1) >= 4)
    outs[...] = jnp.where(upper, gap[4:5, 0:1].reshape(1, 1, 1), mine)
    reduces = []
    for d in range(1, TENSOR):
        to = lax.rem(t + d, TENSOR)
        cp = remote(outs.at[to], sides.at[t], rsend.at[d - 1], rrecv.at[d - 1], g, to)
        cp.start()
        reduces.append(cp)
    sides[t] = outs[t]
    for cp in reduces:
        cp.wait_recv()
    total = jnp.sum(sides[...], axis=0)
    coeff = -BETA * jax.nn.sigmoid(-BETA * total[:, 64:65])
    fin[...] = jnp.where(iota((8, 128), 1) < 64, coeff * total, 0.0)

    ends = []
    for d in range(1, GROUPS):
        ends.append(remote(fin, rowed.at[g], psend.at[d - 1], precv.at[d - 1], lax.rem(g + d, GROUPS), t))
    for d in range(1, TENSOR):
        ends.append(remote(fin, coled.at[g, column_part], csend.at[d], crecv.at[g, column_part], column_group, lax.rem(t + d, TENSOR)))
    for d in range(1, TENSOR):
        ends.append(remote(fin, every.at[t], gsend.at[d - 1], grecv.at[d - 1], g, lax.rem(t + d, TENSOR)))
    for cp in ends:
        cp.start()
    own_column = remote(fin, coled.at[g, column_part], csend.at[0], crecv.at[g, column_part], column_group, t)
    pl.when(column_group != g)(own_column.start)

    @pl.when(column_group == g)
    def _():
        coled[g, column_part] = fin[...]

    rowed[g] = fin[...]
    every[t] = fin[...]

    for d in range(1, GROUPS):
        ends[d - 1].wait_recv()
    for d in range(GROUPS):
        for h in range(2):
            of = lax.rem(g + d, GROUPS)
            cp = remote(fin, coled.at[of, h], csend.at[0], crecv.at[of, h], column_group, t)
            if d == 0:
                pl.when(2 * g + h != t)(cp.wait_recv)
            else:
                cp.wait_recv()

    for cp in ends[-(TENSOR - 1) :]:
        cp.wait_recv()
    ends_o[0:8] = rowed[...]
    ends_o[8:24] = coled[...].reshape(TENSOR, 8, 128)
    ends_o[24:40] = every[...]

    pl.when(column_group != g)(own_column.wait_send)
    for cp in ends + reduces + gathers:
        cp.wait_send()

    @pl.loop(0, pairs)
    def _(q):
        for hop in range(2):
            for i in range(4):
                second(q, i, hop).wait_send()

    if pairs > PRE:
        for hop in range(2):
            for i in range(4):
                ahead(i, hop).wait_send()


def main(pairs, sign, insum, gap, pout, own, g1, pick, gate, upo, w):
    vmem = pl.BlockSpec(memory_space=pltpu.VMEM)
    hbm = pl.BlockSpec(memory_space=pl.ANY)
    dma = pltpu.SemaphoreType.DMA
    return pl.pallas_call(
        functools.partial(main_kernel, pairs),
        out_shape=jax.ShapeDtypeStruct((40, 8, 128), F32),
        in_specs=[vmem] * 4 + [hbm] * 6,
        out_specs=vmem,
        scratch_shapes=[
            pltpu.VMEM((2, pairs, 4, 4, ROWS, 128), BF16),
            pltpu.VMEM((HIDDEN, MODEL), BF16),
            pltpu.VMEM((HIDDEN, TOKENS), BF16),
            pltpu.VMEM((HIDDEN, TOKENS), BF16),
            pltpu.VMEM((pairs * PAIR, TOKENS), BF16),
            pltpu.VMEM((HIDDEN, pairs * PAIR), F32),
            pltpu.VMEM((2 * PAIR, MODEL), BF16),
            pltpu.VMEM((HIDDEN, 2 * PAIR), BF16),
            pltpu.VMEM((TENSOR, 8, 128), F32),
            pltpu.VMEM((RANK, 128), F32),
            pltpu.VMEM((TENSOR, 8, 128), F32),
            pltpu.VMEM((TENSOR, 32, 128), BF16),
            pltpu.VMEM((8, 128), F32),
            pltpu.VMEM((TENSOR, 8, 128), F32),
            pltpu.VMEM((GROUPS, 8, 128), F32),
            pltpu.VMEM((GROUPS, 2, 8, 128), F32),
            dma((11,)),
            dma((TENSOR - 1,)),
            dma((TENSOR - 1,)),
            dma((8,)),
            dma((8,)),
            dma((pairs, 8)),
            dma((pairs, 8)),
            dma((TENSOR - 1,)),
            dma((TENSOR - 1,)),
            dma((TENSOR - 1,)),
            dma((TENSOR - 1,)),
            dma((GROUPS - 1,)),
            dma((GROUPS - 1,)),
            dma((TENSOR,)),
            dma((GROUPS, 2)),
        ],
        compiler_params=pltpu.CompilerParams(collective_id=pairs, has_side_effects=True, vmem_limit_bytes=60 << 20),
        cost_estimate=pl.CostEstimate(flops=3_200_000_000 * pairs, bytes_accessed=30_000_000, transcendentals=8),
        name=f"gather_{pairs}",
    )(sign, insum, gap, pout, own, g1, pick, gate, upo, w)


def final_kernel(ends, grads_o, fisher_o):
    def joined(at, i):
        lanes = iota((GROUPS, 128), 1) < 64
        got = []
        for p in range(2):
            one, two = ends[at, p * 4 + i], ends[at, p * 4 + i + 1]
            got.append(jnp.where(lanes, one, pltpu.roll(two, 64, 1)))
        return got

    columns = [joined(pl.ds(8 + h, GROUPS, 2), i) for h in range(2) for i in (0, 2)]
    rows = [joined(slice(0, GROUPS), i) for i in (0, 2)]
    right = jnp.concatenate([jnp.concatenate(pair, 0) for pair in columns], 1)
    left = jnp.concatenate([jnp.concatenate(pair, 0) for pair in rows], 1)
    fisher_o[...] = lax.dot_general(left, right, TN, precision=lax.Precision.HIGHEST, preferred_element_type=F32)
    lanes = iota((2, 128), 1) < 64
    for c in range(TENSOR):
        tile = ends[24 + c]
        for i in (0, 2):
            one = jnp.concatenate([tile[i : i + 1], tile[4 + i : 5 + i]], 0)
            two = jnp.concatenate([tile[i + 1 : i + 2], tile[5 + i : 6 + i]], 0)
            at = c * 256 + i * 64
            grads_o[:, at : at + 128] = jnp.where(lanes, one, pltpu.roll(two, 64, 1))


def final(ends):
    sds = jax.ShapeDtypeStruct
    vmem = pl.BlockSpec(memory_space=pltpu.VMEM)
    return pl.pallas_call(
        final_kernel,
        out_shape=(sds((2, RANK * RANK), F32), sds((256, 512), F32)),
        in_specs=[vmem],
        out_specs=(vmem, vmem),
        cost_estimate=pl.CostEstimate(flops=4_000_000, bytes_accessed=700_000, transcendentals=0),
        name="final",
    )(ends)


def per_device(
    activations, upstream, gate_pre, up_out, w_down, proj_in, proj_out, policy_logp, ref_logp, loss_mask, resp_len, pair_perm, chosen_first
):
    own, g1, pick, sign, insum, count, gap = stage(
        pair_perm, chosen_first, resp_len, loss_mask, policy_logp, ref_logp, upstream.T, activations.T, proj_in
    )
    args = (sign, insum, gap, proj_out, own, g1, pick, gate_pre.T, up_out.T, w_down)
    if len(SIZES) == 1:
        return final(main(SIZES[0], *args))
    need = (count[0, 0] + PAIR - 1) // PAIR
    index = jnp.zeros((), I32)
    for size in SIZES[:-1]:
        index += jnp.where(need > size, 1, 0)
    return final(lax.switch(index, [functools.partial(main, size) for size in SIZES], *args))


SIZES = (8,)


def solution(mesh):
    placed = (
        P("dp", "tensor"),
        P("dp", "tensor"),
        P("dp", "tensor"),
        P("dp", "tensor"),
        P("tensor", None),
        P(None, "tensor"),
        P(None, "tensor"),
        P("dp", "tensor"),
        P("dp", "tensor"),
        P("dp", None),
        P("dp"),
        P("dp", None),
        P("dp"),
    )
    return jax.shard_map(
        per_device,
        mesh=mesh,
        in_specs=placed,
        out_specs=(P("dp", None), P("tensor", "dp")),
        check_vma=False,
    )
```

```python
import functools

import jax
import jax.numpy as jnp
from jax import lax
from jax.experimental import pallas as pl
from jax.experimental.pallas import tpu as pltpu
from jax.sharding import PartitionSpec as P

BETA = 0.1
F32, BF16, I32 = jnp.float32, jnp.bfloat16, jnp.int32
MESH = pl.DeviceIdType.MESH
NT = (((1,), (1,)), ((), ()))
TN = (((0,), (0,)), ((), ()))

TENSOR = 16
GROUPS = 8
SEQS = 4
LEN = 256
TOKENS = SEQS * LEN
RANK = 64
FEATURES = 320
HIDDEN = 1728
MODEL = TENSOR * FEATURES
CHUNK = 64
ROWS = 160
HALF = 80
PAIR = 2 * CHUNK
ALL_PAIRS = TOKENS // PAIR
SIZES = (4, 5, 6, 7, 8)
PRE = 4


def iota(shape, axis):
    return lax.broadcasted_iota(I32, shape, axis)


def place():
    g, t = lax.axis_index("dp"), lax.axis_index("tensor")
    return g, t, t // 4, t % 4


def stepped(v, by):
    return lax.rem(v + by + 4, 4)


def remote(src, dst, send, recv, g, t):
    return pltpu.make_async_remote_copy(
        src_ref=src, dst_ref=dst, send_sem=send, recv_sem=recv, device_id={"dp": g, "tensor": t}, device_id_type=MESH
    )


def neighbour(axis, by, x, z):
    return stepped(x, by) * 4 + z if axis == 0 else x * 4 + stepped(z, by)


def pair_sign(perm, first, pair, seq):
    side = jnp.where(first[pair] == 1, 1.0, -1.0).astype(F32)
    is_a = jnp.where(perm[0, 2 * pair] == seq, 1.0, 0.0).astype(F32)
    is_b = jnp.where(perm[0, 2 * pair + 1] == seq, 1.0, 0.0).astype(F32)
    return side * (is_a - is_b)


def stage_kernel(
    perm, first, resp, mask, pol, ref, up, act, pin,
    own_o, g1_o, pick_o, sign_o, insum_o, count_o, gap_o,
    pick, cols, own, packed, part, parts, counts, mine,
    keep, ssend, srecv, isend, irecv, csend, crecv,
):
    g, t, x, z = place()
    barrier = pltpu.get_barrier_semaphore()
    for d in range(1, TENSOR):
        pl.semaphore_signal(barrier, inc=1, device_id={"dp": g, "tensor": lax.rem(t + d, TENSOR)}, device_id_type=MESH)
    for d in range(1, GROUPS):
        pl.semaphore_signal(barrier, inc=1, device_id={"dp": lax.rem(g + d, GROUPS), "tensor": t}, device_id_type=MESH)

    row4 = iota((SEQS, LEN), 0)
    start = jnp.zeros((SEQS, LEN), I32)
    for s in range(SEQS):
        start = jnp.where(row4 == s, LEN - resp[s], start)
    live = (iota((SEQS, LEN), 1) >= start) & (mask[...] == 1)
    live_f = jnp.where(live, 1.0, 0.0).astype(F32)
    upto = jnp.where(iota((LEN, LEN), 0) <= iota((LEN, LEN), 1), 1.0, 0.0).astype(BF16)
    running = jnp.dot(live_f.astype(BF16), upto, preferred_element_type=F32)
    begins = [jnp.zeros((1, 1), F32)]
    for s in range(SEQS):
        begins.append(begins[s] + running[s : s + 1, LEN - 1 : LEN])
    for s in range(SEQS):
        at = jnp.where(live[s : s + 1, :], running[s : s + 1, :] - 1.0 + begins[s], -1.0).astype(I32)
        pick[:, s * LEN : (s + 1) * LEN] = jnp.where(iota((TOKENS, LEN), 0) == at, 1.0, 0.0).astype(BF16)
    mine[...] = jnp.broadcast_to(begins[SEQS], (8, 128))

    odd = lax.rem(t, 2)
    r, c = iota((512, FEATURES), 1), iota((512, FEATURES), 0)
    wide = (c < 256) & (r == c + 64 * odd)
    base = jnp.where(odd == 1, 0, 256)
    low = (c >= 256) & (c < 384) & (c - 256 - 64 * odd >= 0) & (c - 256 - 64 * odd < 64) & (r == base + c - 256 - 64 * odd)
    other = 64 * (1 - odd)
    high = (c >= 384) & (c - 384 - other >= 0) & (c - 384 - other < 64) & (r == base + c - 384 - other)
    order = jnp.where(wide | low | high, 1.0, 0.0).astype(BF16)
    cols[...] = jnp.dot(order, up[...], preferred_element_type=F32).astype(BF16)

    def fill(q):
        rows = pl.ds(pl.multiple_of(q * PAIR, PAIR), PAIR)
        moved = lax.dot_general(pick[rows, :], cols[...], NT, preferred_element_type=F32)
        for par in range(2):
            lo = par * CHUNK
            own[par, q, 0:64, :] = moved[lo : lo + 64, 0:128].astype(BF16)
            own[par, q, 64:128, :] = moved[lo : lo + 64, 128:256].astype(BF16)
            own[par, q, 128:160, :] = (moved[lo : lo + 32, 256:384] + moved[lo + 32 : lo + 64, 384:512]).astype(BF16)

    pl.loop(0, PRE)(fill)
    pl.semaphore_wait(barrier, TENSOR - 1 + GROUPS - 1)

    hop1, hop2 = [], []
    for par in range(2):
        slot = x if par == 0 else z
        for k, by in enumerate((1, -1)):
            i = par * 2 + k
            to = neighbour(par, by, x, z)
            hop1.append(remote(own.at[par, 0:PRE], g1_o.at[par, :, slot], ssend.at[i], srecv.at[i], g, to))
            held = g1_o.at[par, :, stepped(slot, -by), k * HALF : (k + 1) * HALF]
            hop2.append(remote(held, held, ssend.at[4 + i], srecv.at[4 + i], g, to))
    for cp in hop1:
        cp.start()
    tells = []
    for d in range(1, GROUPS):
        cp = remote(mine, counts.at[g], csend.at[d - 1], crecv.at[d - 1], lax.rem(g + d, GROUPS), t)
        cp.start()
        tells.append(cp)

    pl.loop(PRE, ALL_PAIRS)(fill)
    keeps = [pltpu.make_async_copy(own, own_o, keep.at[0]), pltpu.make_async_copy(pick, pick_o, keep.at[3])]
    for par in range(2):
        slot = x if par == 0 else z
        keeps.append(pltpu.make_async_copy(own.at[par, 0:PRE], g1_o.at[par, :, slot], keep.at[1 + par]))
    for cp in keeps:
        cp.start()

    packed[...] = lax.dot_general(pick[...], act[...], NT, preferred_element_type=F32).astype(BF16)
    none = jnp.zeros((RANK, FEATURES), BF16)
    sides = lax.dot_general(packed[0:512, :], jnp.concatenate([pin[...], none], 0), NT, preferred_element_type=F32)
    sides += lax.dot_general(packed[512:1024, :], jnp.concatenate([none, pin[...]], 0), NT, preferred_element_type=F32)
    part[...] = sides.reshape(TENSOR, 32, 128)
    halves = []
    for d in range(1, TENSOR):
        to = lax.rem(t + d, TENSOR)
        cp = remote(part.at[to], parts.at[t], isend.at[d - 1], irecv.at[d - 1], g, to)
        cp.start()
        halves.append(cp)

    for cp in hop1:
        cp.wait_recv()
    for cp in hop2:
        cp.start()

    k_at = iota((TOKENS, 128), 0)
    pair_at = lax.rem(iota((TOKENS, 128), 1) // 4, 2)
    sign = jnp.zeros((TOKENS, 128), F32)
    for s in range(SEQS):
        inside = (k_at >= begins[s].astype(I32)) & (k_at < begins[s + 1].astype(I32))
        value = jnp.where(pair_at == 0, pair_sign(perm, first, 0, s), pair_sign(perm, first, 1, s))
        sign = jnp.where(inside, value, sign)
    sign_o[...] = sign.astype(BF16)

    span = jnp.where(iota((LEN, 16), 0) == t * 16 + iota((LEN, 16), 1), 1.0, 0.0).astype(BF16)
    weights = jnp.dot(live_f.astype(BF16), span, preferred_element_type=F32)
    margin = jnp.sum(weights * (pol[...] - ref[...]), axis=1, keepdims=True)
    gaps = []
    for p in range(2):
        gap = jnp.zeros((1, 1), F32)
        for s in range(SEQS):
            gap += pair_sign(perm, first, p, s) * margin[s : s + 1, :]
        gaps.append(gap)
    gap_o[...] = jnp.where(iota((8, 128), 0) < 4, gaps[0], gaps[1])

    for cp in halves:
        cp.wait_recv()
    parts[t] = part[t]
    total = parts[0]
    for i in range(1, TENSOR):
        total += parts[i]
    insum_o[...] = total.astype(BF16)
    for cp in tells:
        cp.wait_recv()
    counts[g] = mine[...]
    most = counts[0]
    for i in range(1, GROUPS):
        most = jnp.maximum(most, counts[i])
    most = jnp.max(most)
    index = jnp.zeros((), I32)
    for size in SIZES[:-1]:
        index += jnp.where(most > size * PAIR, 1, 0)
    count_o[0] = index
    for cp in hop2:
        cp.wait_recv()
    for cp in hop1 + hop2 + halves + tells:
        cp.wait_send()
    for cp in keeps:
        cp.wait()


def stage(perm, first, resp, mask, pol, ref, up, act, pin):
    sds = jax.ShapeDtypeStruct
    vmem = pl.BlockSpec(memory_space=pltpu.VMEM)
    smem = pl.BlockSpec(memory_space=pltpu.SMEM)
    hbm = pl.BlockSpec(memory_space=pl.ANY)
    dma = pltpu.SemaphoreType.DMA
    return pl.pallas_call(
        stage_kernel,
        out_shape=(
            sds((2, ALL_PAIRS, ROWS, 128), BF16),
            sds((2, PRE, 4, ROWS, 128), BF16),
            sds((TOKENS, TOKENS), BF16),
            sds((TOKENS, 128), BF16),
            sds((32, 128), BF16),
            sds((1,), I32),
            sds((8, 128), F32),
        ),
        in_specs=[smem] * 3 + [vmem] * 6,
        out_specs=(hbm, hbm, hbm, vmem, vmem, smem, vmem),
        scratch_shapes=[
            pltpu.VMEM((TOKENS, TOKENS), BF16),
            pltpu.VMEM((512, TOKENS), BF16),
            pltpu.VMEM((2, ALL_PAIRS, ROWS, 128), BF16),
            pltpu.VMEM((TOKENS, FEATURES), BF16),
            pltpu.VMEM((TENSOR, 32, 128), F32),
            pltpu.VMEM((TENSOR, 32, 128), F32),
            pltpu.VMEM((GROUPS, 8, 128), F32),
            pltpu.VMEM((8, 128), F32),
            dma((4,)),
            dma((8,)),
            dma((8,)),
            dma((TENSOR - 1,)),
            dma((TENSOR - 1,)),
            dma((GROUPS - 1,)),
            dma((GROUPS - 1,)),
        ],
        compiler_params=pltpu.CompilerParams(collective_id=0, has_side_effects=True, vmem_limit_bytes=56 << 20),
        cost_estimate=pl.CostEstimate(flops=2_000_000_000, bytes_accessed=8_000_000, transcendentals=0),
        name="stage",
    )(perm, first, resp, mask, pol, ref, up, act, pin)


def main_kernel(
    pairs, sign, insum, gap, pout, own_h, g1_h, pick_h, gate_h, upo_h, w_h,
    ends_o,
    blocks, w, gate, upo, pick, m, u, grad, sides, diff, outs, ins, fin, every, rowed, coled,
    load, asend, arecv, fsend, frecv, ssend, srecv, rsend, rrecv, gsend, grecv, psend, precv, csend, crecv,
):
    g, t, x, z = place()
    column_group, column_part = t // 2, lax.rem(t, 2)
    barrier = pltpu.get_barrier_semaphore()
    for d in range(1, TENSOR):
        pl.semaphore_signal(barrier, inc=1, device_id={"dp": g, "tensor": lax.rem(t + d, TENSOR)}, device_id_type=MESH)
    for d in range(1, GROUPS):
        pl.semaphore_signal(barrier, inc=1, device_id={"dp": lax.rem(g + d, GROUPS), "tensor": t}, device_id_type=MESH)
    for d in range(GROUPS):
        for h in range(2):
            of, at = lax.rem(g + d, GROUPS), 2 * g + h

            def greet(of=of, at=at):
                pl.semaphore_signal(barrier, inc=1, device_id={"dp": of, "tensor": at}, device_id_type=MESH)

            if d == 0:
                pl.when(at != t)(greet)
            else:
                greet()

    wide = MODEL // 4
    loads = []
    halves = [
        pltpu.make_async_copy(pick_h.at[0 : pairs * PAIR], pick, load.at[9]),
        pltpu.make_async_copy(gate_h, gate, load.at[0]),
        pltpu.make_async_copy(upo_h, upo, load.at[10]),
    ]
    for par in range(2):
        to = blocks.at[0, 0:PRE, :, z] if par == 0 else blocks.at[1, 0:PRE, x]
        loads.append(pltpu.make_async_copy(g1_h.at[par], to, load.at[1 + par]))
        if pairs > PRE:
            loads.append(pltpu.make_async_copy(own_h.at[par, PRE:pairs], blocks.at[par, PRE:pairs, x, z], load.at[3 + par]))
    w_loads = [pltpu.make_async_copy(w_h.at[:, i * wide : (i + 1) * wide], w.at[:, i * wide : (i + 1) * wide], load.at[5 + i]) for i in range(4)]
    for cp in loads + halves + w_loads:
        cp.start()
    mates = TENSOR - 1 + GROUPS - 1 + TENSOR
    pl.semaphore_wait(barrier, mates - jnp.where(column_group == g, 1, 0))
    for cp in loads:
        cp.wait()

    def second(q, i, hop):
        par, k = i // 2, i % 2
        by = 1 if k == 0 else -1
        if par == 0:
            to = neighbour(1, by, x, z)
            ref = blocks.at[0, q, :, z] if hop == 0 else blocks.at[0, q, :, stepped(z, -by), k * HALF : (k + 1) * HALF]
        else:
            to = neighbour(0, by, x, z)
            ref = blocks.at[1, q, x] if hop == 0 else blocks.at[1, q, stepped(x, -by), :, k * HALF : (k + 1) * HALF]
        return remote(ref, ref, ssend.at[q, hop * 4 + i], srecv.at[q, hop * 4 + i], g, to)

    def ahead(i, hop):
        par, k = i // 2, i % 2
        by = 1 if k == 0 else -1
        to = neighbour(par, by, x, z)
        if hop == 0:
            ref = blocks.at[par, PRE:pairs, x, z]
        elif par == 0:
            ref = blocks.at[0, PRE:pairs, stepped(x, -by), z, k * HALF : (k + 1) * HALF]
        else:
            ref = blocks.at[1, PRE:pairs, x, stepped(z, -by), k * HALF : (k + 1) * HALF]
        return remote(ref, ref, fsend.at[hop * 4 + i], frecv.at[hop * 4 + i], g, to)

    for q in range(2):
        for i in range(4):
            second(q, i, 0).start()
    if pairs > PRE:
        for i in range(4):
            ahead(i, 0).start()
    ins[t] = insum[...]
    gathers = []
    for d in range(1, TENSOR):
        cp = remote(insum, ins.at[t], asend.at[d - 1], arecv.at[d - 1], g, lax.rem(t + d, TENSOR))
        cp.start()
        gathers.append(cp)
    diff[...] = jnp.zeros_like(diff)
    for cp in halves:
        cp.wait()

    def factor(first_pair, count):
        rows = pl.ds(pl.multiple_of(first_pair * PAIR, PAIR), count * PAIR)

        @pl.loop(0, HIDDEN // 432)
        def _(i):
            units = pl.ds(pl.multiple_of(i * 432, 16), 432)
            v = lax.dot_general(gate[units, :], pick[rows, :], NT, preferred_element_type=F32)
            o = lax.dot_general(upo[units, :], pick[rows, :], NT, preferred_element_type=F32)
            sig = jax.nn.sigmoid(v)
            m[units, rows] = o * sig * (1.0 + v * (1.0 - sig))

    def compute(first_pair, count):
        tokens = count * PAIR
        lanes = iota((32, 128), 1) < 64
        for one in range(count):
            q = first_pair + one
            for par in range(2):
                for s in range(TENSOR // 2):
                    a, b = blocks.at[par, q, s // 2, 2 * (s % 2)], blocks.at[par, q, s // 2, 2 * (s % 2) + 1]
                    r, c = one * PAIR + par * CHUNK, s * 640
                    u[r : r + 64, c : c + 128] = a[0:64, :]
                    u[r : r + 64, c + 128 : c + 256] = a[64:128, :]
                    u[r : r + 64, c + 384 : c + 512] = b[0:64, :]
                    u[r : r + 64, c + 512 : c + 640] = b[64:128, :]
                    left, right = a[128:160, :].astype(F32), b[128:160, :].astype(F32)
                    u[r : r + 32, c + 256 : c + 384] = jnp.where(lanes, left, right).astype(BF16)
                    u[r + 32 : r + 64, c + 256 : c + 384] = pltpu.roll(jnp.where(lanes, right, left), 64, 1).astype(BF16)
        rows = pl.ds(pl.multiple_of(first_pair * PAIR, PAIR), tokens)

        @pl.loop(0, HIDDEN // 576)
        def _(i):
            units = pl.ds(pl.multiple_of(i * 576, 16), 576)
            acc = None
            for k in range(4):
                at = slice(k * wide, (k + 1) * wide)
                more = lax.dot_general(w[units, at], u[0:tokens, at], NT, preferred_element_type=F32)
                acc = more if acc is None else acc + more
            grad[units, 0:tokens] = (acc * m[units, rows]).astype(BF16)

        out_side = jnp.dot(pout[...], grad[:, 0:tokens], preferred_element_type=F32)
        r, c = iota((128, 128), 0), iota((128, 128), 1)
        for one in range(count):
            q = first_pair + one
            side_rows = pl.ds(pl.multiple_of(lax.rem(q, 4) * 4, 4), 4)
            spread = jnp.where(r == jnp.where(q >= 4, 64, 0) + (c // 8) * 4 + lax.rem(c, 4), 1.0, 0.0).astype(BF16)
            in_side = jnp.dot(ins[side_rows].reshape(PAIR, 128), spread, preferred_element_type=F32)
            signed = in_side * sign[pl.ds(pl.multiple_of(q * PAIR, PAIR), PAIR), :].astype(F32)
            part = out_side[:, one * PAIR : (one + 1) * PAIR]
            diff[...] += jnp.dot(part, signed, precision=lax.Precision.HIGHEST, preferred_element_type=F32)

    def turn(q):
        for i in range(4):
            second(q, i, 0).wait_recv()
        for i in range(4):
            second(q, i, 1).start()

    def send(q):
        for i in range(4):
            second(q, i, 0).start()

    full, rest = pairs // 2, pairs % 2
    factor(0, 2)

    @pl.loop(0, full + 1)
    def _(n):
        @pl.when(2 * n < pairs)
        def _():
            turn(2 * n)

        if pairs > PRE:

            @pl.when(n == 0)
            def _():
                for i in range(4):
                    ahead(i, 0).wait_recv()
                for i in range(4):
                    ahead(i, 1).start()

            @pl.when(n == 1)
            def _():
                for i in range(4):
                    ahead(i, 1).wait_recv()

        @pl.when(2 * n + 2 < pairs)
        def _():
            send(2 * n + 2)

        @pl.when(n + 1 < full)
        def _():
            factor(2 * n + 2, 2)

        if rest:

            @pl.when(n + 1 == full)
            def _():
                factor(2 * full, 1)

        @pl.when(2 * n + 1 < pairs)
        def _():
            turn(2 * n + 1)

        @pl.when(2 * n + 3 < pairs)
        def _():
            send(2 * n + 3)

        @pl.when(n == 1)
        def _():
            for cp in w_loads:
                cp.wait()
            for cp in gathers:
                cp.wait_recv()

        @pl.when(n >= 1)
        def _():
            for one in range(2):
                for i in range(4):
                    second(2 * n - 2 + one, i, 1).wait_recv()
            compute(2 * n - 2, 2)

    if rest:
        for i in range(4):
            second(pairs - 1, i, 1).wait_recv()
        compute(pairs - 1, 1)

    mine = jnp.concatenate([diff[...].T, jnp.broadcast_to(gap[0:1, 0:1], (128, 64))], 1).reshape(TENSOR, 8, 128)
    upper = (iota((TENSOR, 8, 128), 2) >= 64) & (iota((TENSOR, 8, 128), 1) >= 4)
    outs[...] = jnp.where(upper, gap[4:5, 0:1].reshape(1, 1, 1), mine)
    reduces = []
    for d in range(1, TENSOR):
        to = lax.rem(t + d, TENSOR)
        cp = remote(outs.at[to], sides.at[t], rsend.at[d - 1], rrecv.at[d - 1], g, to)
        cp.start()
        reduces.append(cp)
    sides[t] = outs[t]
    for cp in reduces:
        cp.wait_recv()
    total = jnp.sum(sides[...], axis=0)
    coeff = -BETA * jax.nn.sigmoid(-BETA * total[:, 64:65])
    fin[...] = jnp.where(iota((8, 128), 1) < 64, coeff * total, 0.0)

    ends = []
    for d in range(1, GROUPS):
        ends.append(remote(fin, rowed.at[g], psend.at[d - 1], precv.at[d - 1], lax.rem(g + d, GROUPS), t))
    for d in range(1, TENSOR):
        ends.append(remote(fin, coled.at[g, column_part], csend.at[d], crecv.at[g, column_part], column_group, lax.rem(t + d, TENSOR)))
    for d in range(1, TENSOR):
        ends.append(remote(fin, every.at[t], gsend.at[d - 1], grecv.at[d - 1], g, lax.rem(t + d, TENSOR)))
    for cp in ends:
        cp.start()
    own_column = remote(fin, coled.at[g, column_part], csend.at[0], crecv.at[g, column_part], column_group, t)
    pl.when(column_group != g)(own_column.start)

    @pl.when(column_group == g)
    def _():
        coled[g, column_part] = fin[...]

    rowed[g] = fin[...]
    every[t] = fin[...]

    for d in range(1, GROUPS):
        ends[d - 1].wait_recv()
    for d in range(GROUPS):
        for h in range(2):
            of = lax.rem(g + d, GROUPS)
            cp = remote(fin, coled.at[of, h], csend.at[0], crecv.at[of, h], column_group, t)
            if d == 0:
                pl.when(2 * g + h != t)(cp.wait_recv)
            else:
                cp.wait_recv()

    for cp in ends[-(TENSOR - 1) :]:
        cp.wait_recv()
    ends_o[0:8] = rowed[...]
    ends_o[8:24] = coled[...].reshape(TENSOR, 8, 128)
    ends_o[24:40] = every[...]

    pl.when(column_group != g)(own_column.wait_send)
    for cp in ends + reduces + gathers:
        cp.wait_send()

    @pl.loop(0, pairs)
    def _(q):
        for hop in range(2):
            for i in range(4):
                second(q, i, hop).wait_send()

    if pairs > PRE:
        for hop in range(2):
            for i in range(4):
                ahead(i, hop).wait_send()


def main(pairs, sign, insum, gap, pout, own, g1, pick, gate, upo, w):
    vmem = pl.BlockSpec(memory_space=pltpu.VMEM)
    hbm = pl.BlockSpec(memory_space=pl.ANY)
    dma = pltpu.SemaphoreType.DMA
    return pl.pallas_call(
        functools.partial(main_kernel, pairs),
        out_shape=jax.ShapeDtypeStruct((40, 8, 128), F32),
        in_specs=[vmem] * 4 + [hbm] * 6,
        out_specs=vmem,
        scratch_shapes=[
            pltpu.VMEM((2, pairs, 4, 4, ROWS, 128), BF16),
            pltpu.VMEM((HIDDEN, MODEL), BF16),
            pltpu.VMEM((HIDDEN, TOKENS), BF16),
            pltpu.VMEM((HIDDEN, TOKENS), BF16),
            pltpu.VMEM((pairs * PAIR, TOKENS), BF16),
            pltpu.VMEM((HIDDEN, pairs * PAIR), F32),
            pltpu.VMEM((2 * PAIR, MODEL), BF16),
            pltpu.VMEM((HIDDEN, 2 * PAIR), BF16),
            pltpu.VMEM((TENSOR, 8, 128), F32),
            pltpu.VMEM((RANK, 128), F32),
            pltpu.VMEM((TENSOR, 8, 128), F32),
            pltpu.VMEM((TENSOR, 32, 128), BF16),
            pltpu.VMEM((8, 128), F32),
            pltpu.VMEM((TENSOR, 8, 128), F32),
            pltpu.VMEM((GROUPS, 8, 128), F32),
            pltpu.VMEM((GROUPS, 2, 8, 128), F32),
            dma((11,)),
            dma((TENSOR - 1,)),
            dma((TENSOR - 1,)),
            dma((8,)),
            dma((8,)),
            dma((pairs, 8)),
            dma((pairs, 8)),
            dma((TENSOR - 1,)),
            dma((TENSOR - 1,)),
            dma((TENSOR - 1,)),
            dma((TENSOR - 1,)),
            dma((GROUPS - 1,)),
            dma((GROUPS - 1,)),
            dma((TENSOR,)),
            dma((GROUPS, 2)),
        ],
        compiler_params=pltpu.CompilerParams(collective_id=pairs, has_side_effects=True, vmem_limit_bytes=60 << 20),
        cost_estimate=pl.CostEstimate(flops=3_200_000_000 * pairs, bytes_accessed=30_000_000, transcendentals=8),
        name=f"gather_{pairs}",
    )(sign, insum, gap, pout, own, g1, pick, gate, upo, w)


def final_kernel(ends, grads_o, fisher_o):
    def joined(at, i):
        lanes = iota((GROUPS, 128), 1) < 64
        got = []
        for p in range(2):
            one, two = ends[at, p * 4 + i], ends[at, p * 4 + i + 1]
            got.append(jnp.where(lanes, one, pltpu.roll(two, 64, 1)))
        return got

    columns = [joined(pl.ds(8 + h, GROUPS, 2), i) for h in range(2) for i in (0, 2)]
    rows = [joined(slice(0, GROUPS), i) for i in (0, 2)]
    right = jnp.concatenate([jnp.concatenate(pair, 0) for pair in columns], 1)
    left = jnp.concatenate([jnp.concatenate(pair, 0) for pair in rows], 1)
    fisher_o[...] = lax.dot_general(left, right, TN, precision=lax.Precision.HIGHEST, preferred_element_type=F32)
    lanes = iota((2, 128), 1) < 64
    for c in range(TENSOR):
        tile = ends[24 + c]
        for i in (0, 2):
            one = jnp.concatenate([tile[i : i + 1], tile[4 + i : 5 + i]], 0)
            two = jnp.concatenate([tile[i + 1 : i + 2], tile[5 + i : 6 + i]], 0)
            at = c * 256 + i * 64
            grads_o[:, at : at + 128] = jnp.where(lanes, one, pltpu.roll(two, 64, 1))


def final(ends):
    sds = jax.ShapeDtypeStruct
    vmem = pl.BlockSpec(memory_space=pltpu.VMEM)
    return pl.pallas_call(
        final_kernel,
        out_shape=(sds((2, RANK * RANK), F32), sds((256, 512), F32)),
        in_specs=[vmem],
        out_specs=(vmem, vmem),
        cost_estimate=pl.CostEstimate(flops=4_000_000, bytes_accessed=700_000, transcendentals=0),
        name="final",
    )(ends)


def per_device(
    activations, upstream, gate_pre, up_out, w_down, proj_in, proj_out, policy_logp, ref_logp, loss_mask, resp_len, pair_perm, chosen_first
):
    own, g1, pick, sign, insum, count, gap = stage(
        pair_perm, chosen_first, resp_len, loss_mask, policy_logp, ref_logp, upstream.T, activations.T, proj_in
    )
    args = (sign, insum, gap, proj_out, own, g1, pick, gate_pre.T, up_out.T, w_down)
    if len(SIZES) == 1:
        return final(main(SIZES[0], *args))
    return final(lax.switch(count[0], [functools.partial(main, size) for size in SIZES], *args))


def solution(mesh):
    placed = (
        P("dp", "tensor"),
        P("dp", "tensor"),
        P("dp", "tensor"),
        P("dp", "tensor"),
        P("tensor", None),
        P(None, "tensor"),
        P(None, "tensor"),
        P("dp", "tensor"),
        P("dp", "tensor"),
        P("dp", None),
        P("dp"),
        P("dp", None),
        P("dp"),
    )
    return jax.shard_map(
        per_device,
        mesh=mesh,
        in_specs=placed,
        out_specs=(P("dp", None), P("tensor", "dp")),
        check_vma=False,
    )
```

```python
import functools

import jax
import jax.numpy as jnp
from jax import lax
from jax.experimental import pallas as pl
from jax.experimental.pallas import tpu as pltpu
from jax.sharding import PartitionSpec as P

BETA = 0.1
F32, BF16, I32 = jnp.float32, jnp.bfloat16, jnp.int32
MESH = pl.DeviceIdType.MESH
NT = (((1,), (1,)), ((), ()))
TN = (((0,), (0,)), ((), ()))

TENSOR = 16
GROUPS = 8
SEQS = 4
LEN = 256
TOKENS = SEQS * LEN
RANK = 64
FEATURES = 320
HIDDEN = 1728
MODEL = TENSOR * FEATURES
CHUNK = 64
WIDE = 2 * CHUNK
ROWS = WIDE + CHUNK // 2
PAIR = 2 * CHUNK
ALL_PAIRS = TOKENS // PAIR
PRE = 512 // PAIR
GROUP = 256 // PAIR
LOOK = 2
SIZES = (4, 5, 6, 7, 8)


def cut(parity):
    return ROWS // 2 if ROWS % 32 == 0 else ROWS // 2 + (8 if parity == 0 else -8)


def iota(shape, axis):
    return lax.broadcasted_iota(I32, shape, axis)


def place():
    g, t = lax.axis_index("dp"), lax.axis_index("tensor")
    return g, t, t // 4, t % 4


def stepped(v, by):
    return lax.rem(v + by + 4, 4)


def remote(src, dst, send, recv, g, t):
    return pltpu.make_async_remote_copy(
        src_ref=src, dst_ref=dst, send_sem=send, recv_sem=recv, device_id={"dp": g, "tensor": t}, device_id_type=MESH
    )


def neighbour(axis, by, x, z):
    return stepped(x, by) * 4 + z if axis == 0 else x * 4 + stepped(z, by)


def greet(g, t):
    barrier = pltpu.get_barrier_semaphore()
    for d in range(1, TENSOR):
        pl.semaphore_signal(barrier, inc=1, device_id={"dp": g, "tensor": lax.rem(t + d, TENSOR)}, device_id_type=MESH)
    for d in range(1, GROUPS):
        pl.semaphore_signal(barrier, inc=1, device_id={"dp": lax.rem(g + d, GROUPS), "tensor": t}, device_id_type=MESH)
    return barrier


def pair_sign(perm, first, pair, seq):
    side = jnp.where(first[pair] == 1, 1.0, -1.0).astype(F32)
    is_a = jnp.where(perm[0, 2 * pair] == seq, 1.0, 0.0).astype(F32)
    is_b = jnp.where(perm[0, 2 * pair + 1] == seq, 1.0, 0.0).astype(F32)
    return side * (is_a - is_b)


def stage_kernel(
    perm, first, resp, mask, pol, ref, up_h, act_h, pin_h,
    own_o, g1_o, pick_o, sign_o, insum_o, count_o, gap_o,
    pick, cols, own, packed, part, parts, counts, mine, up, act, pin,
    load, keep, ssend, srecv, isend, irecv, csend, crecv,
):
    g, t, x, z = place()
    barrier = greet(g, t)
    loads = [pltpu.make_async_copy(*refs, load.at[i]) for i, refs in enumerate(((up_h, up), (act_h, act), (pin_h, pin)))]
    for cp in loads:
        cp.start()

    row4 = iota((SEQS, LEN), 0)
    start = jnp.zeros((SEQS, LEN), I32)
    for s in range(SEQS):
        start = jnp.where(row4 == s, LEN - resp[s], start)
    live = (iota((SEQS, LEN), 1) >= start) & (mask[...] == 1)
    live_f = jnp.where(live, 1.0, 0.0).astype(F32)
    upto = jnp.where(iota((LEN, LEN), 0) <= iota((LEN, LEN), 1), 1.0, 0.0).astype(BF16)
    running = jnp.dot(live_f.astype(BF16), upto, preferred_element_type=F32)
    begins = [jnp.zeros((1, 1), F32)]
    for s in range(SEQS):
        begins.append(begins[s] + running[s : s + 1, LEN - 1 : LEN])

    def choose(half):
        for s in range(SEQS):
            at = jnp.where(live[s : s + 1, :], running[s : s + 1, :] - 1.0 + begins[s], -1.0).astype(I32)
            here = iota((512, LEN), 0) + half * 512 == at
            pick[half * 512 : (half + 1) * 512, s * LEN : (s + 1) * LEN] = jnp.where(here, 1.0, 0.0).astype(BF16)

    choose(0)
    mine[...] = jnp.broadcast_to(begins[SEQS], (8, 128))

    odd = lax.rem(t, 2)
    r, c = iota((512, FEATURES), 1), iota((512, FEATURES), 0)
    wide = (c < 256) & (r == c + 64 * odd)
    base = jnp.where(odd == 1, 0, 256)
    low = (c >= 256) & (c < 384) & (c - 256 - 64 * odd >= 0) & (c - 256 - 64 * odd < 64) & (r == base + c - 256 - 64 * odd)
    other = 64 * (1 - odd)
    high = (c >= 384) & (c - 384 - other >= 0) & (c - 384 - other < 64) & (r == base + c - 384 - other)
    order = jnp.where(wide | low | high, 1.0, 0.0).astype(BF16)
    loads[0].wait()
    cols[...] = jnp.dot(order, up[...], preferred_element_type=F32).astype(BF16)

    def fill(n):
        rows = pl.ds(pl.multiple_of(n * 128, 128), 128)
        moved = lax.dot_general(pick[rows, :], cols[...], NT, preferred_element_type=F32)
        for one in range(128 // PAIR):
            for par in range(2):
                lo, mid, hi = (one * PAIR + par * CHUNK + e for e in (0, CHUNK // 2, CHUNK))
                q = n * (128 // PAIR) + one
                own[par, q, 0:CHUNK, :] = moved[lo:hi, 0:128].astype(BF16)
                own[par, q, CHUNK:WIDE, :] = moved[lo:hi, 128:256].astype(BF16)
                own[par, q, WIDE:ROWS, :] = (moved[lo:mid, 256:384] + moved[mid:hi, 384:512]).astype(BF16)

    hop1, hop2 = [], []
    for half in range(2):
        pairs = slice(half * PRE // 2, (half + 1) * PRE // 2)
        for par in range(2):
            slot = x if par == 0 else z
            for k, by in enumerate((1, -1)):
                i = half * 4 + par * 2 + k
                to = neighbour(par, by, x, z)
                hop1.append(remote(own.at[par, pairs], g1_o.at[par, pairs, slot], ssend.at[i], srecv.at[i], g, to))
                held = g1_o.at[par, pairs, stepped(slot, -by), (0, cut(par))[k] : (cut(par), ROWS)[k]]
                hop2.append(remote(held, held, ssend.at[8 + i], srecv.at[8 + i], g, to))
    pl.loop(0, 2)(fill)
    pl.semaphore_wait(barrier, TENSOR - 1 + GROUPS - 1)
    for cp in hop1[:4]:
        cp.start()
    pl.loop(2, 4)(fill)
    for cp in hop1[4:]:
        cp.start()
    tells = []
    for d in range(1, GROUPS):
        cp = remote(mine, counts.at[g], csend.at[d - 1], crecv.at[d - 1], lax.rem(g + d, GROUPS), t)
        cp.start()
        tells.append(cp)

    choose(1)
    for cp in loads[1:]:
        cp.wait()
    packed[...] = lax.dot_general(pick[...], act[...], NT, preferred_element_type=F32).astype(BF16)
    none = jnp.zeros((RANK, FEATURES), BF16)
    sides = lax.dot_general(packed[0:512, :], jnp.concatenate([pin[...], none], 0), NT, preferred_element_type=F32)
    sides += lax.dot_general(packed[512:1024, :], jnp.concatenate([none, pin[...]], 0), NT, preferred_element_type=F32)
    part[...] = sides.reshape(TENSOR, 32, 128)
    halves = []
    for d in range(1, TENSOR):
        to = lax.rem(t + d, TENSOR)
        cp = remote(part.at[to], parts.at[t], isend.at[d - 1], irecv.at[d - 1], g, to)
        cp.start()
        halves.append(cp)

    for half in range(2):
        for cp in hop1[half * 4 : half * 4 + 4]:
            cp.wait_recv()
        for cp in hop2[half * 4 : half * 4 + 4]:
            cp.start()
    pl.loop(4, 8)(fill)
    keeps = [pltpu.make_async_copy(own, own_o, keep.at[0]), pltpu.make_async_copy(pick, pick_o, keep.at[3])]
    for par in range(2):
        slot = x if par == 0 else z
        keeps.append(pltpu.make_async_copy(own.at[par, 0:PRE], g1_o.at[par, :, slot], keep.at[1 + par]))
    for cp in keeps:
        cp.start()

    k_at = iota((TOKENS, 128), 0)
    pair_at = lax.rem(iota((TOKENS, 128), 1) // 4, 2)
    sign = jnp.zeros((TOKENS, 128), F32)
    for s in range(SEQS):
        inside = (k_at >= begins[s].astype(I32)) & (k_at < begins[s + 1].astype(I32))
        value = jnp.where(pair_at == 0, pair_sign(perm, first, 0, s), pair_sign(perm, first, 1, s))
        sign = jnp.where(inside, value, sign)
    sign_o[...] = sign.astype(BF16)

    span = jnp.where(iota((LEN, 16), 0) == t * 16 + iota((LEN, 16), 1), 1.0, 0.0).astype(BF16)
    weights = jnp.dot(live_f.astype(BF16), span, preferred_element_type=F32)
    margin = jnp.sum(weights * (pol[...] - ref[...]), axis=1, keepdims=True)
    gaps = []
    for p in range(2):
        gap = jnp.zeros((1, 1), F32)
        for s in range(SEQS):
            gap += pair_sign(perm, first, p, s) * margin[s : s + 1, :]
        gaps.append(gap)
    gap_o[...] = jnp.where(iota((8, 128), 0) < 4, gaps[0], gaps[1])

    for cp in halves:
        cp.wait_recv()
    parts[t] = part[t]
    total = parts[0]
    for i in range(1, TENSOR):
        total += parts[i]
    insum_o[...] = total.astype(BF16)
    for cp in tells:
        cp.wait_recv()
    counts[g] = mine[...]
    most = counts[0]
    for i in range(1, GROUPS):
        most = jnp.maximum(most, counts[i])
    most = jnp.max(most)
    index = jnp.zeros((), I32)
    for size in SIZES[:-1]:
        index += jnp.where(most > size * PAIR, 1, 0)
    count_o[0] = index
    for cp in hop2:
        cp.wait_recv()
    for cp in hop1 + hop2 + halves + tells:
        cp.wait_send()
    for cp in keeps:
        cp.wait()


def stage(perm, first, resp, mask, pol, ref, up, act, pin):
    sds = jax.ShapeDtypeStruct
    vmem = pl.BlockSpec(memory_space=pltpu.VMEM)
    smem = pl.BlockSpec(memory_space=pltpu.SMEM)
    hbm = pl.BlockSpec(memory_space=pl.ANY)
    dma = pltpu.SemaphoreType.DMA
    return pl.pallas_call(
        stage_kernel,
        out_shape=(
            sds((2, ALL_PAIRS, ROWS, 128), BF16),
            sds((2, PRE, 4, ROWS, 128), BF16),
            sds((TOKENS, TOKENS), BF16),
            sds((TOKENS, 128), BF16),
            sds((32, 128), BF16),
            sds((1,), I32),
            sds((8, 128), F32),
        ),
        in_specs=[smem] * 3 + [vmem] * 3 + [hbm] * 3,
        out_specs=(hbm, hbm, hbm, vmem, vmem, smem, vmem),
        scratch_shapes=[
            pltpu.VMEM((TOKENS, TOKENS), BF16),
            pltpu.VMEM((512, TOKENS), BF16),
            pltpu.VMEM((2, ALL_PAIRS, ROWS, 128), BF16),
            pltpu.VMEM((TOKENS, FEATURES), BF16),
            pltpu.VMEM((TENSOR, 32, 128), F32),
            pltpu.VMEM((TENSOR, 32, 128), F32),
            pltpu.VMEM((GROUPS, 8, 128), F32),
            pltpu.VMEM((8, 128), F32),
            pltpu.VMEM((FEATURES, TOKENS), BF16),
            pltpu.VMEM((FEATURES, TOKENS), BF16),
            pltpu.VMEM((RANK, FEATURES), BF16),
            dma((3,)),
            dma((4,)),
            dma((16,)),
            dma((16,)),
            dma((TENSOR - 1,)),
            dma((TENSOR - 1,)),
            dma((GROUPS - 1,)),
            dma((GROUPS - 1,)),
        ],
        compiler_params=pltpu.CompilerParams(collective_id=0, has_side_effects=True, vmem_limit_bytes=56 << 20),
        cost_estimate=pl.CostEstimate(flops=2_000_000_000, bytes_accessed=8_000_000, transcendentals=0),
        name="stage",
    )(perm, first, resp, mask, pol, ref, up, act, pin)


def main_kernel(
    pairs, gap, insum_h, sign_h, pout_h, own_h, g1_h, pick_h, gate_h, upo_h, w_h,
    ends_o,
    blocks, w, gate, upo, pick, sign, pout, m, u, grad, sides, diff, outs, ins, fin, every, rowed, coled,
    load, asend, arecv, fsend, frecv, ssend, srecv, rsend, rrecv, gsend, grecv, psend, precv, csend, crecv,
):
    g, t, x, z = place()
    column_group, column_part = t // 2, lax.rem(t, 2)
    skip = pairs % GROUP
    total = skip + pairs
    early = skip + PRE
    groups = total // GROUP
    barrier = greet(g, t)
    for d in range(GROUPS):
        for h in range(2):
            of, at = lax.rem(g + d, GROUPS), 2 * g + h

            def tell(of=of, at=at):
                pl.semaphore_signal(barrier, inc=1, device_id={"dp": of, "tensor": at}, device_id_type=MESH)

            if d == 0:
                pl.when(at != t)(tell)
            else:
                tell()

    wide = MODEL // 4
    first_loads = []
    for par in range(2):
        to = blocks.at[0, skip:early, :, z] if par == 0 else blocks.at[1, skip:early, x]
        first_loads.append(pltpu.make_async_copy(g1_h.at[par], to, load.at[par]))
        if pairs > PRE:
            first_loads.append(pltpu.make_async_copy(own_h.at[par, PRE:pairs], blocks.at[par, early:total, x, z], load.at[2 + par]))
    first_loads.append(pltpu.make_async_copy(insum_h, ins.at[t], load.at[4]))
    factor_loads = [
        pltpu.make_async_copy(pick_h.at[0 : pairs * PAIR], pick.at[skip * PAIR : total * PAIR], load.at[5]),
        pltpu.make_async_copy(gate_h, gate, load.at[6]),
        pltpu.make_async_copy(upo_h, upo, load.at[7]),
    ]
    last_loads = [pltpu.make_async_copy(sign_h.at[0 : pairs * PAIR], sign.at[skip * PAIR : total * PAIR], load.at[8]), pltpu.make_async_copy(pout_h, pout, load.at[9])]
    for i in range(4):
        at = slice(i * wide, (i + 1) * wide)
        last_loads.append(pltpu.make_async_copy(w_h.at[:, at], w.at[:, at], load.at[10 + i]))
    for cp in first_loads + factor_loads + last_loads:
        cp.start()
    mates = TENSOR - 1 + GROUPS - 1 + TENSOR
    pl.semaphore_wait(barrier, mates - jnp.where(column_group == g, 1, 0))
    for cp in first_loads:
        cp.wait()

    def part_of(k, parity):
        return slice(0, cut(parity)) if k == 0 else slice(cut(parity), ROWS)

    def second(q, i, hop, parity=0):
        par, k = i // 2, i % 2
        by = 1 if k == 0 else -1
        if par == 0:
            to = neighbour(1, by, x, z)
            ref = blocks.at[0, q, :, z] if hop == 0 else blocks.at[0, q, :, stepped(z, -by), part_of(k, parity)]
        else:
            to = neighbour(0, by, x, z)
            ref = blocks.at[1, q, x] if hop == 0 else blocks.at[1, q, stepped(x, -by), :, part_of(k, parity)]
        return remote(ref, ref, ssend.at[q, hop * 4 + i], srecv.at[q, hop * 4 + i], g, to)

    def ahead(i, hop):
        par, k = i // 2, i % 2
        by = 1 if k == 0 else -1
        to = neighbour(par, by, x, z)
        if hop == 0:
            ref = blocks.at[par, early:total, x, z]
        elif par == 0:
            ref = blocks.at[0, early:total, stepped(x, -by), z, part_of(k, 0)]
        else:
            ref = blocks.at[1, early:total, x, stepped(z, -by), part_of(k, 1)]
        return remote(ref, ref, fsend.at[hop * 4 + i], frecv.at[hop * 4 + i], g, to)

    def send(q):
        for i in range(4):
            second(q, i, 0).start()

    def turn(q, parity):
        for i in range(4):
            second(q, i, 0).wait_recv()
        for i in range(4):
            second(q, i, 1, parity).start()

    def arrive(q, parity):
        for i in range(4):
            second(q, i, 1, parity).wait_recv()

    if pairs > PRE:
        for i in range(4):
            ahead(i, 0).start()
    send(skip)
    gathers = []
    for d in range(1, TENSOR):
        cp = remote(ins.at[t], ins.at[t], asend.at[d - 1], arecv.at[d - 1], g, lax.rem(t + d, TENSOR))
        cp.start()
        gathers.append(cp)
    for q in range(skip + 1, skip + LOOK):
        send(q)
    diff[...] = jnp.zeros_like(diff)
    if skip:
        pick[0:PAIR, :] = jnp.zeros((PAIR, TOKENS), BF16)
        sign[0:PAIR, :] = jnp.zeros((PAIR, 128), BF16)
        u[0:PAIR, :] = jnp.zeros((PAIR, MODEL), BF16)

    def tokens_of(n, count):
        return pl.ds(pl.multiple_of(n * GROUP * PAIR, PAIR), count * PAIR)

    def factor(n, count):
        rows = tokens_of(n, count)

        @pl.loop(0, HIDDEN // 432)
        def _(i):
            units = pl.ds(pl.multiple_of(i * 432, 16), 432)
            v = lax.dot_general(gate[units, :], pick[rows, :], NT, preferred_element_type=F32)
            o = lax.dot_general(upo[units, :], pick[rows, :], NT, preferred_element_type=F32)
            sig = jax.nn.sigmoid(v)
            m[units, rows] = o * sig * (1.0 + v * (1.0 - sig))

    def assemble(q, one):
        lanes = iota((CHUNK // 2, 128), 1) < 64
        for par in range(2):
            for s in range(TENSOR // 2):
                a, b = blocks.at[par, q, s // 2, 2 * (s % 2)], blocks.at[par, q, s // 2, 2 * (s % 2) + 1]
                c, base = s * 640, one * PAIR + par * CHUNK
                whole = pl.ds(pl.multiple_of(base, CHUNK), CHUNK)
                u[whole, c : c + 128] = a[0:CHUNK, :]
                u[whole, c + 128 : c + 256] = a[CHUNK:WIDE, :]
                u[whole, c + 384 : c + 512] = b[0:CHUNK, :]
                u[whole, c + 512 : c + 640] = b[CHUNK:WIDE, :]
                left, right = a[WIDE:ROWS, :].astype(F32), b[WIDE:ROWS, :].astype(F32)
                half = CHUNK // 2
                front, back = pl.ds(pl.multiple_of(base, half), half), pl.ds(pl.multiple_of(base + half, half), half)
                u[front, c + 256 : c + 384] = jnp.where(lanes, left, right).astype(BF16)
                u[back, c + 256 : c + 384] = pltpu.roll(jnp.where(lanes, right, left), 64, 1).astype(BF16)

    def multiply(n, count, i):
        units = pl.ds(pl.multiple_of(i * 576, 16), 576)
        acc = None
        for k in range(4):
            at = slice(k * wide, (k + 1) * wide)
            more = lax.dot_general(w[units, at], u[0 : count * PAIR, at], NT, preferred_element_type=F32)
            acc = more if acc is None else acc + more
        grad[units, 0 : count * PAIR] = (acc * m[units, tokens_of(n, count)]).astype(BF16)

    def project(n, count):
        out_side = jnp.dot(pout[...], grad[:, 0 : count * PAIR], preferred_element_type=F32)
        high = out_side.astype(BF16)
        low = (out_side - high.astype(F32)).astype(BF16)
        both = jnp.dot(jnp.concatenate([high, low], 0), sign[tokens_of(n, count), :], preferred_element_type=F32)
        diff[...] += both[0:RANK] + both[RANK:]

    def sign_sides():
        r, c = iota((128, 128), 0), iota((128, 128), 1)

        @pl.loop(0, pairs * PAIR // 64)
        def _(n):
            at = pl.ds(pl.multiple_of(lax.rem(n, 8) * 2, 2), 2)
            spread = jnp.where(r == jnp.where(n >= 8, 64, 0) + (c // 8) * 4 + lax.rem(c, 4), 1.0, 0.0).astype(BF16)
            in_side = jnp.dot(ins[at].reshape(64, 128), spread, preferred_element_type=F32)
            rows = pl.ds(pl.multiple_of(skip * PAIR + n * 64, 64), 64)
            sign[rows, :] = (in_side * sign[rows, :].astype(F32)).astype(BF16)

    for cp in factor_loads:
        cp.wait()
    factor(0, GROUP)

    def gather_in(n):
        for e in range(GROUP):
            pl.when(n * GROUP + e >= skip)(lambda e=e: arrive(n * GROUP + e, e))

        @pl.loop(0, GROUP)
        def _(e):
            pl.when(n * GROUP + e >= skip)(lambda: assemble(n * GROUP + e, e))

    def pass_on(q, parity):
        pl.when((q >= skip) & (q < total))(lambda: turn(q, parity))
        if pairs > PRE and parity == skip:

            @pl.when(q == skip)
            def _():
                for i in range(4):
                    ahead(i, 0).wait_recv()
                for i in range(4):
                    ahead(i, 1).start()

            @pl.when(q + LOOK == early)
            def _():
                for i in range(4):
                    ahead(i, 1).wait_recv()

        pl.when((q >= skip) & (q + LOOK < total))(lambda: send(q + LOOK))

    @pl.loop(0, groups + 1)
    def _(n):
        pass_on(n * GROUP, 0)
        pl.when(n >= 1)(lambda: gather_in(n - 1))

        @pl.loop(0, 3)
        def _(i):
            pl.when(n >= 1)(lambda: multiply(n - 1, GROUP, i))

            @pl.when(i == 0)
            def _():
                if skip:
                    pass_on(n * GROUP + 1, 1)
                pl.when(n == 0)(lambda: factor(1, GROUP))
                if not skip:
                    pass_on(n * GROUP + 1, 1)

        pl.when(n >= 1)(lambda: project(n - 1, GROUP))

        @pl.when(n == 0)
        def _():
            for cp in gathers:
                cp.wait_recv()
            for cp in last_loads:
                cp.wait()
            sign_sides()

        pl.when(n + 2 < groups)(lambda: factor(n + 2, GROUP))

    mine = jnp.concatenate([diff[...].T, jnp.broadcast_to(gap[0:1, 0:1], (128, 64))], 1).reshape(TENSOR, 8, 128)
    upper = (iota((TENSOR, 8, 128), 2) >= 64) & (iota((TENSOR, 8, 128), 1) >= 4)
    outs[...] = jnp.where(upper, gap[4:5, 0:1].reshape(1, 1, 1), mine)
    reduces = []
    for d in range(1, TENSOR):
        to = lax.rem(t + d, TENSOR)
        cp = remote(outs.at[to], sides.at[t], rsend.at[d - 1], rrecv.at[d - 1], g, to)
        cp.start()
        reduces.append(cp)
    sides[t] = outs[t]
    for cp in reduces:
        cp.wait_recv()
    summed = jnp.sum(sides[...], axis=0)
    coeff = -BETA * jax.nn.sigmoid(-BETA * summed[:, 64:65])
    fin[...] = jnp.where(iota((8, 128), 1) < 64, coeff * summed, 0.0)

    ends = []
    for d in range(1, GROUPS):
        ends.append(remote(fin, rowed.at[g], psend.at[d - 1], precv.at[d - 1], lax.rem(g + d, GROUPS), t))
    for d in range(1, TENSOR):
        ends.append(remote(fin, coled.at[g, column_part], csend.at[d], crecv.at[g, column_part], column_group, lax.rem(t + d, TENSOR)))
    for d in range(1, TENSOR):
        ends.append(remote(fin, every.at[t], gsend.at[d - 1], grecv.at[d - 1], g, lax.rem(t + d, TENSOR)))
    for cp in ends:
        cp.start()
    own_column = remote(fin, coled.at[g, column_part], csend.at[0], crecv.at[g, column_part], column_group, t)
    pl.when(column_group != g)(own_column.start)

    @pl.when(column_group == g)
    def _():
        coled[g, column_part] = fin[...]

    rowed[g] = fin[...]
    every[t] = fin[...]

    for d in range(1, GROUPS):
        ends[d - 1].wait_recv()
    for d in range(GROUPS):
        for h in range(2):
            of = lax.rem(g + d, GROUPS)
            cp = remote(fin, coled.at[of, h], csend.at[0], crecv.at[of, h], column_group, t)
            if d == 0:
                pl.when(2 * g + h != t)(cp.wait_recv)
            else:
                cp.wait_recv()

    for cp in ends[-(TENSOR - 1) :]:
        cp.wait_recv()
    ends_o[0:8] = rowed[...]
    ends_o[8:24] = coled[...].reshape(TENSOR, 8, 128)
    ends_o[24:40] = every[...]

    pl.when(column_group != g)(own_column.wait_send)
    for cp in ends + reduces + gathers:
        cp.wait_send()

    @pl.loop(skip, total)
    def _(q):
        for i in range(4):
            second(q, i, 0).wait_send()

    for q in range(skip, total):
        for i in range(4):
            second(q, i, 1, q % 2).wait_send()

    if pairs > PRE:
        for hop in range(2):
            for i in range(4):
                ahead(i, hop).wait_send()


def main(pairs, gap, insum, sign, pout, own, g1, pick, gate, upo, w):
    total = pairs + pairs % GROUP
    vmem = pl.BlockSpec(memory_space=pltpu.VMEM)
    hbm = pl.BlockSpec(memory_space=pl.ANY)
    dma = pltpu.SemaphoreType.DMA
    return pl.pallas_call(
        functools.partial(main_kernel, pairs),
        out_shape=jax.ShapeDtypeStruct((40, 8, 128), F32),
        in_specs=[vmem] + [hbm] * 9,
        out_specs=vmem,
        scratch_shapes=[
            pltpu.VMEM((2, total, 4, 4, ROWS, 128), BF16),
            pltpu.VMEM((HIDDEN, MODEL), BF16),
            pltpu.VMEM((HIDDEN, TOKENS), BF16),
            pltpu.VMEM((HIDDEN, TOKENS), BF16),
            pltpu.VMEM((total * PAIR, TOKENS), BF16),
            pltpu.VMEM((total * PAIR, 128), BF16),
            pltpu.VMEM((RANK, HIDDEN), BF16),
            pltpu.VMEM((HIDDEN, total * PAIR), F32),
            pltpu.VMEM((GROUP * PAIR, MODEL), BF16),
            pltpu.VMEM((HIDDEN, GROUP * PAIR), BF16),
            pltpu.VMEM((TENSOR, 8, 128), F32),
            pltpu.VMEM((RANK, 128), F32),
            pltpu.VMEM((TENSOR, 8, 128), F32),
            pltpu.VMEM((TENSOR, 32, 128), BF16),
            pltpu.VMEM((8, 128), F32),
            pltpu.VMEM((TENSOR, 8, 128), F32),
            pltpu.VMEM((GROUPS, 8, 128), F32),
            pltpu.VMEM((GROUPS, 2, 8, 128), F32),
            dma((14,)),
            dma((TENSOR - 1,)),
            dma((TENSOR - 1,)),
            dma((8,)),
            dma((8,)),
            dma((total, 8)),
            dma((total, 8)),
            dma((TENSOR - 1,)),
            dma((TENSOR - 1,)),
            dma((TENSOR - 1,)),
            dma((TENSOR - 1,)),
            dma((GROUPS - 1,)),
            dma((GROUPS - 1,)),
            dma((TENSOR,)),
            dma((GROUPS, 2)),
        ],
        compiler_params=pltpu.CompilerParams(collective_id=pairs, has_side_effects=True, vmem_limit_bytes=60 << 20),
        cost_estimate=pl.CostEstimate(flops=25_000_000 * PAIR * pairs, bytes_accessed=30_000_000, transcendentals=8),
        name=f"gather_{pairs}",
    )(gap, insum, sign, pout, own, g1, pick, gate, upo, w)


def final_kernel(ends, grads_o, fisher_o):
    def joined(at, i):
        lanes = iota((GROUPS, 128), 1) < 64
        got = []
        for p in range(2):
            one, two = ends[at, p * 4 + i], ends[at, p * 4 + i + 1]
            got.append(jnp.where(lanes, one, pltpu.roll(two, 64, 1)))
        return got

    columns = [joined(pl.ds(8 + h, GROUPS, 2), i) for h in range(2) for i in (0, 2)]
    rows = [joined(slice(0, GROUPS), i) for i in (0, 2)]
    right = jnp.concatenate([jnp.concatenate(pair, 0) for pair in columns], 1)
    left = jnp.concatenate([jnp.concatenate(pair, 0) for pair in rows], 1)
    fisher_o[...] = lax.dot_general(left, right, TN, precision=lax.Precision.HIGHEST, preferred_element_type=F32)
    lanes = iota((2, 128), 1) < 64
    for c in range(TENSOR):
        tile = ends[24 + c]
        for i in (0, 2):
            one = jnp.concatenate([tile[i : i + 1], tile[4 + i : 5 + i]], 0)
            two = jnp.concatenate([tile[i + 1 : i + 2], tile[5 + i : 6 + i]], 0)
            at = c * 256 + i * 64
            grads_o[:, at : at + 128] = jnp.where(lanes, one, pltpu.roll(two, 64, 1))


def final(ends):
    sds = jax.ShapeDtypeStruct
    vmem = pl.BlockSpec(memory_space=pltpu.VMEM)
    return pl.pallas_call(
        final_kernel,
        out_shape=(sds((2, RANK * RANK), F32), sds((256, 512), F32)),
        in_specs=[vmem],
        out_specs=(vmem, vmem),
        cost_estimate=pl.CostEstimate(flops=4_000_000, bytes_accessed=700_000, transcendentals=0),
        name="final",
    )(ends)


def per_device(
    activations, upstream, gate_pre, up_out, w_down, proj_in, proj_out, policy_logp, ref_logp, loss_mask, resp_len, pair_perm, chosen_first
):
    own, g1, pick, sign, insum, count, gap = stage(
        pair_perm, chosen_first, resp_len, loss_mask, policy_logp, ref_logp, upstream.T, activations.T, proj_in
    )
    args = (gap, insum, sign, proj_out, own, g1, pick, gate_pre.T, up_out.T, w_down)
    if len(SIZES) == 1:
        return final(main(SIZES[0], *args))
    return final(lax.switch(count[0], [functools.partial(main, size) for size in SIZES], *args))


def solution(mesh):
    placed = (
        P("dp", "tensor"),
        P("dp", "tensor"),
        P("dp", "tensor"),
        P("dp", "tensor"),
        P("tensor", None),
        P(None, "tensor"),
        P(None, "tensor"),
        P("dp", "tensor"),
        P("dp", "tensor"),
        P("dp", None),
        P("dp"),
        P("dp", None),
        P("dp"),
    )
    return jax.shard_map(
        per_device,
        mesh=mesh,
        in_specs=placed,
        out_specs=(P("dp", None), P("tensor", "dp")),
        check_vma=False,
    )
```

```python
import functools

import jax
import jax.numpy as jnp
from jax import lax
from jax.experimental import pallas as pl
from jax.experimental.pallas import tpu as pltpu
from jax.sharding import PartitionSpec as P

BETA = 0.1
F32, BF16, I32 = jnp.float32, jnp.bfloat16, jnp.int32
MESH = pl.DeviceIdType.MESH
NT = (((1,), (1,)), ((), ()))
TN = (((0,), (0,)), ((), ()))

TENSOR = 16
GROUPS = 8
SEQS = 4
LEN = 256
TOKENS = SEQS * LEN
RANK = 64
FEATURES = 320
HIDDEN = 1728
MODEL = TENSOR * FEATURES
CHUNK = 64
WIDE = 2 * CHUNK
ROWS = WIDE + CHUNK // 2
PAIR = 2 * CHUNK
ALL_PAIRS = TOKENS // PAIR
PRE = 512 // PAIR
GROUP = 256 // PAIR
LOOK = 2
SIZES = (4, 5, 6, 7, 8)


FAR = (10, 6, 14, 9, 11, 2, 8, 5, 7, 13, 15, 1, 3, 4, 12)


def cut(parity):
    return ROWS // 2 if ROWS % 32 == 0 else ROWS // 2 + (8 if parity == 0 else -8)


def iota(shape, axis):
    return lax.broadcasted_iota(I32, shape, axis)


def place():
    g, t = lax.axis_index("dp"), lax.axis_index("tensor")
    return g, t, t // 4, t % 4


def stepped(v, by):
    return lax.rem(v + by + 4, 4)


def remote(src, dst, send, recv, g, t):
    return pltpu.make_async_remote_copy(
        src_ref=src, dst_ref=dst, send_sem=send, recv_sem=recv, device_id={"dp": g, "tensor": t}, device_id_type=MESH
    )


def neighbour(axis, by, x, z):
    return stepped(x, by) * 4 + z if axis == 0 else x * 4 + stepped(z, by)


def greet(g, t):
    barrier = pltpu.get_barrier_semaphore()
    for d in FAR:
        pl.semaphore_signal(barrier, inc=1, device_id={"dp": g, "tensor": lax.rem(t + d, TENSOR)}, device_id_type=MESH)
    for d in range(1, GROUPS):
        pl.semaphore_signal(barrier, inc=1, device_id={"dp": lax.rem(g + d, GROUPS), "tensor": t}, device_id_type=MESH)
    return barrier


def pair_sign(perm, first, pair, seq):
    side = jnp.where(first[pair] == 1, 1.0, -1.0).astype(F32)
    is_a = jnp.where(perm[0, 2 * pair] == seq, 1.0, 0.0).astype(F32)
    is_b = jnp.where(perm[0, 2 * pair + 1] == seq, 1.0, 0.0).astype(F32)
    return side * (is_a - is_b)


def stage_kernel(
    perm, first, resp, mask_h, pol_h, ref_h, up_h, act_h, pin_h,
    own_o, g1_o, pick_o, sign_o, insum_o, count_o, gap_o,
    pick, cols, own, packed, part, parts, counts, mine, up, act, pin, mask, pol, ref,
    load, keep, ssend, srecv, isend, irecv, csend, crecv,
):
    g, t, x, z = place()
    pieces = ((mask_h, mask), (up_h, up), (act_h, act), (pin_h, pin), (pol_h, pol), (ref_h, ref))
    loads = [pltpu.make_async_copy(*refs, load.at[i]) for i, refs in enumerate(pieces)]
    for cp in loads:
        cp.start()
    barrier = greet(g, t)
    loads[0].wait()

    row4 = iota((SEQS, LEN), 0)
    start = jnp.zeros((SEQS, LEN), I32)
    for s in range(SEQS):
        start = jnp.where(row4 == s, LEN - resp[s], start)
    live = (iota((SEQS, LEN), 1) >= start) & (mask[...] == 1)
    live_f = jnp.where(live, 1.0, 0.0).astype(F32)
    upto = jnp.where(iota((LEN, LEN), 0) <= iota((LEN, LEN), 1), 1.0, 0.0).astype(BF16)
    running = jnp.dot(live_f.astype(BF16), upto, preferred_element_type=F32)
    begins = [jnp.zeros((1, 1), F32)]
    for s in range(SEQS):
        begins.append(begins[s] + running[s : s + 1, LEN - 1 : LEN])

    def choose(half):
        for s in range(SEQS):
            at = jnp.where(live[s : s + 1, :], running[s : s + 1, :] - 1.0 + begins[s], -1.0).astype(I32)
            here = iota((512, LEN), 0) + half * 512 == at
            pick[half * 512 : (half + 1) * 512, s * LEN : (s + 1) * LEN] = jnp.where(here, 1.0, 0.0).astype(BF16)

    choose(0)
    mine[...] = jnp.broadcast_to(begins[SEQS], (8, 128))

    odd = lax.rem(t, 2)
    r, c = iota((512, FEATURES), 1), iota((512, FEATURES), 0)
    wide = (c < 256) & (r == c + 64 * odd)
    base = jnp.where(odd == 1, 0, 256)
    low = (c >= 256) & (c < 384) & (c - 256 - 64 * odd >= 0) & (c - 256 - 64 * odd < 64) & (r == base + c - 256 - 64 * odd)
    other = 64 * (1 - odd)
    high = (c >= 384) & (c - 384 - other >= 0) & (c - 384 - other < 64) & (r == base + c - 384 - other)
    order = jnp.where(wide | low | high, 1.0, 0.0).astype(BF16)
    loads[1].wait()
    cols[...] = jnp.dot(order, up[...], preferred_element_type=F32).astype(BF16)

    def fill(n):
        rows = pl.ds(pl.multiple_of(n * 128, 128), 128)
        moved = lax.dot_general(pick[rows, :], cols[...], NT, preferred_element_type=F32)
        for one in range(128 // PAIR):
            for par in range(2):
                lo, mid, hi = (one * PAIR + par * CHUNK + e for e in (0, CHUNK // 2, CHUNK))
                q = n * (128 // PAIR) + one
                own[par, q, 0:CHUNK, :] = moved[lo:hi, 0:128].astype(BF16)
                own[par, q, CHUNK:WIDE, :] = moved[lo:hi, 128:256].astype(BF16)
                own[par, q, WIDE:ROWS, :] = (moved[lo:mid, 256:384] + moved[mid:hi, 384:512]).astype(BF16)

    hop1, hop2 = [], []
    for half in range(2):
        pairs = slice(half * PRE // 2, (half + 1) * PRE // 2)
        for par in range(2):
            slot = x if par == 0 else z
            for k, by in enumerate((1, -1)):
                i = half * 4 + par * 2 + k
                to = neighbour(par, by, x, z)
                hop1.append(remote(own.at[par, pairs], g1_o.at[par, pairs, slot], ssend.at[i], srecv.at[i], g, to))
                held = g1_o.at[par, pairs, stepped(slot, -by), (0, cut(par))[k] : (cut(par), ROWS)[k]]
                hop2.append(remote(held, held, ssend.at[8 + i], srecv.at[8 + i], g, to))
    pl.loop(0, 2)(fill)
    pl.semaphore_wait(barrier, TENSOR - 1 + GROUPS - 1)
    for cp in hop1[:4]:
        cp.start()
    pl.loop(2, 4)(fill)
    for cp in hop1[4:]:
        cp.start()
    tells = []
    for d in range(1, GROUPS):
        cp = remote(mine, counts.at[g], csend.at[d - 1], crecv.at[d - 1], lax.rem(g + d, GROUPS), t)
        cp.start()
        tells.append(cp)

    choose(1)
    for cp in loads[2:]:
        cp.wait()
    packed[...] = lax.dot_general(pick[...], act[...], NT, preferred_element_type=F32).astype(BF16)
    none = jnp.zeros((RANK, FEATURES), BF16)
    sides = lax.dot_general(packed[0:512, :], jnp.concatenate([pin[...], none], 0), NT, preferred_element_type=F32)
    sides += lax.dot_general(packed[512:1024, :], jnp.concatenate([none, pin[...]], 0), NT, preferred_element_type=F32)
    part[...] = sides.reshape(TENSOR, 32, 128)
    halves = []
    for d in FAR:
        to = lax.rem(t + d, TENSOR)
        cp = remote(part.at[to], parts.at[t], isend.at[d - 1], irecv.at[d - 1], g, to)
        cp.start()
        halves.append(cp)

    for half in range(2):
        for cp in hop1[half * 4 : half * 4 + 4]:
            cp.wait_recv()
        for cp in hop2[half * 4 : half * 4 + 4]:
            cp.start()
    pl.loop(4, 8)(fill)
    keeps = [pltpu.make_async_copy(own, own_o, keep.at[0]), pltpu.make_async_copy(pick, pick_o, keep.at[3])]
    for par in range(2):
        slot = x if par == 0 else z
        keeps.append(pltpu.make_async_copy(own.at[par, 0:PRE], g1_o.at[par, :, slot], keep.at[1 + par]))
    for cp in keeps:
        cp.start()

    k_at = iota((TOKENS, 128), 0)
    pair_at = lax.rem(iota((TOKENS, 128), 1) // 4, 2)
    sign = jnp.zeros((TOKENS, 128), F32)
    for s in range(SEQS):
        inside = (k_at >= begins[s].astype(I32)) & (k_at < begins[s + 1].astype(I32))
        value = jnp.where(pair_at == 0, pair_sign(perm, first, 0, s), pair_sign(perm, first, 1, s))
        sign = jnp.where(inside, value, sign)
    sign_o[...] = sign.astype(BF16)

    span = jnp.where(iota((LEN, 16), 0) == t * 16 + iota((LEN, 16), 1), 1.0, 0.0).astype(BF16)
    weights = jnp.dot(live_f.astype(BF16), span, preferred_element_type=F32)
    margin = jnp.sum(weights * (pol[...] - ref[...]), axis=1, keepdims=True)
    gaps = []
    for p in range(2):
        gap = jnp.zeros((1, 1), F32)
        for s in range(SEQS):
            gap += pair_sign(perm, first, p, s) * margin[s : s + 1, :]
        gaps.append(gap)
    gap_o[...] = jnp.where(iota((8, 128), 0) < 4, gaps[0], gaps[1])

    for cp in halves:
        cp.wait_recv()
    parts[t] = part[t]
    total = parts[0]
    for i in range(1, TENSOR):
        total += parts[i]
    insum_o[...] = total.astype(BF16)
    for cp in tells:
        cp.wait_recv()
    counts[g] = mine[...]
    most = counts[0]
    for i in range(1, GROUPS):
        most = jnp.maximum(most, counts[i])
    most = jnp.max(most)
    index = jnp.zeros((), I32)
    for size in SIZES[:-1]:
        index += jnp.where(most > size * PAIR, 1, 0)
    count_o[0] = index
    for cp in hop2:
        cp.wait_recv()
    for cp in hop1 + hop2 + halves + tells:
        cp.wait_send()
    for cp in keeps:
        cp.wait()


def stage(perm, first, resp, mask, pol, ref, up, act, pin):
    sds = jax.ShapeDtypeStruct
    vmem = pl.BlockSpec(memory_space=pltpu.VMEM)
    smem = pl.BlockSpec(memory_space=pltpu.SMEM)
    hbm = pl.BlockSpec(memory_space=pl.ANY)
    dma = pltpu.SemaphoreType.DMA
    return pl.pallas_call(
        stage_kernel,
        out_shape=(
            sds((2, ALL_PAIRS, ROWS, 128), BF16),
            sds((2, PRE, 4, ROWS, 128), BF16),
            sds((TOKENS, TOKENS), BF16),
            sds((TOKENS, 128), BF16),
            sds((32, 128), BF16),
            sds((1,), I32),
            sds((8, 128), F32),
        ),
        in_specs=[smem] * 3 + [hbm] * 6,
        out_specs=(hbm, hbm, hbm, vmem, vmem, smem, vmem),
        scratch_shapes=[
            pltpu.VMEM((TOKENS, TOKENS), BF16),
            pltpu.VMEM((512, TOKENS), BF16),
            pltpu.VMEM((2, ALL_PAIRS, ROWS, 128), BF16),
            pltpu.VMEM((TOKENS, FEATURES), BF16),
            pltpu.VMEM((TENSOR, 32, 128), F32),
            pltpu.VMEM((TENSOR, 32, 128), F32),
            pltpu.VMEM((GROUPS, 8, 128), F32),
            pltpu.VMEM((8, 128), F32),
            pltpu.VMEM((FEATURES, TOKENS), BF16),
            pltpu.VMEM((FEATURES, TOKENS), BF16),
            pltpu.VMEM((RANK, FEATURES), BF16),
            pltpu.VMEM((SEQS, LEN), I32),
            pltpu.VMEM((SEQS, 16), F32),
            pltpu.VMEM((SEQS, 16), F32),
            dma((6,)),
            dma((4,)),
            dma((16,)),
            dma((16,)),
            dma((TENSOR - 1,)),
            dma((TENSOR - 1,)),
            dma((GROUPS - 1,)),
            dma((GROUPS - 1,)),
        ],
        compiler_params=pltpu.CompilerParams(collective_id=0, has_side_effects=True, vmem_limit_bytes=56 << 20),
        cost_estimate=pl.CostEstimate(flops=2_000_000_000, bytes_accessed=8_000_000, transcendentals=0),
        name="stage",
    )(perm, first, resp, mask, pol, ref, up, act, pin)


def main_kernel(
    pairs, gap, insum_h, sign_h, pout_h, own_h, g1_h, pick_h, gate_h, upo_h, w_h,
    ends_o,
    blocks, w, gate, upo, pick, sign, pout, m, u, grad, sides, diff, outs, ins, fin, every, rowed, coled,
    load, asend, arecv, fsend, frecv, ssend, srecv, rsend, rrecv, gsend, grecv, psend, precv, csend, crecv,
):
    g, t, x, z = place()
    column_group, column_part = t // 2, lax.rem(t, 2)
    skip = pairs % GROUP
    total = skip + pairs
    early = skip + PRE
    groups = total // GROUP
    wide = MODEL // 4
    first_loads = []
    for par in range(2):
        to = blocks.at[0, skip:early, :, z] if par == 0 else blocks.at[1, skip:early, x]
        first_loads.append(pltpu.make_async_copy(g1_h.at[par], to, load.at[par]))
        if pairs > PRE:
            first_loads.append(pltpu.make_async_copy(own_h.at[par, PRE:pairs], blocks.at[par, early:total, x, z], load.at[2 + par]))
    first_loads.append(pltpu.make_async_copy(insum_h, ins.at[t], load.at[4]))
    factor_loads = [
        pltpu.make_async_copy(pick_h.at[0 : pairs * PAIR], pick.at[skip * PAIR : total * PAIR], load.at[5]),
        pltpu.make_async_copy(gate_h, gate, load.at[6]),
        pltpu.make_async_copy(upo_h, upo, load.at[7]),
    ]
    last_loads = [pltpu.make_async_copy(sign_h.at[0 : pairs * PAIR], sign.at[skip * PAIR : total * PAIR], load.at[8]), pltpu.make_async_copy(pout_h, pout, load.at[9])]
    for i in range(4):
        at = slice(i * wide, (i + 1) * wide)
        last_loads.append(pltpu.make_async_copy(w_h.at[:, at], w.at[:, at], load.at[10 + i]))
    for cp in first_loads:
        cp.start()
    barrier = greet(g, t)
    for d in range(GROUPS):
        for h in range(2):
            of, at = lax.rem(g + d, GROUPS), 2 * g + h

            def tell(of=of, at=at):
                pl.semaphore_signal(barrier, inc=1, device_id={"dp": of, "tensor": at}, device_id_type=MESH)

            if d == 0:
                pl.when(at != t)(tell)
            else:
                tell()

    for cp in factor_loads + last_loads:
        cp.start()
    mates = TENSOR - 1 + GROUPS - 1 + TENSOR
    pl.semaphore_wait(barrier, mates - jnp.where(column_group == g, 1, 0))
    for cp in first_loads:
        cp.wait()

    def part_of(k, parity):
        return slice(0, cut(parity)) if k == 0 else slice(cut(parity), ROWS)

    def second(q, i, hop, parity=0):
        par, k = i // 2, i % 2
        by = 1 if k == 0 else -1
        if par == 0:
            to = neighbour(1, by, x, z)
            ref = blocks.at[0, q, :, z] if hop == 0 else blocks.at[0, q, :, stepped(z, -by), part_of(k, parity)]
        else:
            to = neighbour(0, by, x, z)
            ref = blocks.at[1, q, x] if hop == 0 else blocks.at[1, q, stepped(x, -by), :, part_of(k, parity)]
        return remote(ref, ref, ssend.at[q, hop * 4 + i], srecv.at[q, hop * 4 + i], g, to)

    def ahead(i, hop):
        par, k = i // 2, i % 2
        by = 1 if k == 0 else -1
        to = neighbour(par, by, x, z)
        if hop == 0:
            ref = blocks.at[par, early:total, x, z]
        elif par == 0:
            ref = blocks.at[0, early:total, stepped(x, -by), z, part_of(k, 0)]
        else:
            ref = blocks.at[1, early:total, x, stepped(z, -by), part_of(k, 1)]
        return remote(ref, ref, fsend.at[hop * 4 + i], frecv.at[hop * 4 + i], g, to)

    def send(q):
        for i in range(4):
            second(q, i, 0).start()

    def turn(q, parity):
        for i in range(4):
            second(q, i, 0).wait_recv()
            second(q, i, 1, parity).start()

    def arrive(q, parity):
        for i in range(4):
            second(q, i, 1, parity).wait_recv()

    if pairs > PRE:
        for i in range(4):
            ahead(i, 0).start()
    send(skip)
    gathers = []
    for d in FAR:
        cp = remote(ins.at[t], ins.at[t], asend.at[d - 1], arecv.at[d - 1], g, lax.rem(t + d, TENSOR))
        cp.start()
        gathers.append(cp)
    for q in range(skip + 1, skip + LOOK):
        send(q)
    diff[...] = jnp.zeros_like(diff)
    if skip:
        pick[0:PAIR, :] = jnp.zeros((PAIR, TOKENS), BF16)
        sign[0:PAIR, :] = jnp.zeros((PAIR, 128), BF16)
        u[0:PAIR, :] = jnp.zeros((PAIR, MODEL), BF16)

    def tokens_of(n, count):
        return pl.ds(pl.multiple_of(n * GROUP * PAIR, PAIR), count * PAIR)

    def factor(n, count):
        rows = tokens_of(n, count)

        @pl.loop(0, HIDDEN // 432)
        def _(i):
            units = pl.ds(pl.multiple_of(i * 432, 16), 432)
            v = lax.dot_general(gate[units, :], pick[rows, :], NT, preferred_element_type=F32)
            o = lax.dot_general(upo[units, :], pick[rows, :], NT, preferred_element_type=F32)
            sig = jax.nn.sigmoid(v)
            m[units, rows] = o * sig * (1.0 + v * (1.0 - sig))

    def assemble(q, one):
        lanes = iota((CHUNK // 2, 128), 1) < 64
        for par in range(2):
            for s in range(TENSOR // 2):
                a, b = blocks.at[par, q, s // 2, 2 * (s % 2)], blocks.at[par, q, s // 2, 2 * (s % 2) + 1]
                c, base = s * 640, one * PAIR + par * CHUNK
                whole = pl.ds(pl.multiple_of(base, CHUNK), CHUNK)
                u[whole, c : c + 128] = a[0:CHUNK, :]
                u[whole, c + 128 : c + 256] = a[CHUNK:WIDE, :]
                u[whole, c + 384 : c + 512] = b[0:CHUNK, :]
                u[whole, c + 512 : c + 640] = b[CHUNK:WIDE, :]
                left, right = a[WIDE:ROWS, :].astype(F32), b[WIDE:ROWS, :].astype(F32)
                half = CHUNK // 2
                front, back = pl.ds(pl.multiple_of(base, half), half), pl.ds(pl.multiple_of(base + half, half), half)
                u[front, c + 256 : c + 384] = jnp.where(lanes, left, right).astype(BF16)
                u[back, c + 256 : c + 384] = pltpu.roll(jnp.where(lanes, right, left), 64, 1).astype(BF16)

    def multiply(n, count, i):
        units = pl.ds(pl.multiple_of(i * 864, 16), 864)
        acc = None
        for k in range(4):
            at = slice(k * wide, (k + 1) * wide)
            more = lax.dot_general(w[units, at], u[0 : count * PAIR, at], NT, preferred_element_type=F32)
            acc = more if acc is None else acc + more
        grad[units, 0 : count * PAIR] = (acc * m[units, tokens_of(n, count)]).astype(BF16)

    def project(n, count):
        out_side = jnp.dot(pout[...], grad[:, 0 : count * PAIR], preferred_element_type=F32)
        high = out_side.astype(BF16)
        low = (out_side - high.astype(F32)).astype(BF16)
        both = jnp.dot(jnp.concatenate([high, low], 0), sign[tokens_of(n, count), :], preferred_element_type=F32)
        diff[...] += both[0:RANK] + both[RANK:]

    def sign_sides():
        r, c = iota((128, 128), 0), iota((128, 128), 1)

        @pl.loop(0, pairs * PAIR // 64)
        def _(n):
            at = pl.ds(pl.multiple_of(lax.rem(n, 8) * 2, 2), 2)
            spread = jnp.where(r == jnp.where(n >= 8, 64, 0) + (c // 8) * 4 + lax.rem(c, 4), 1.0, 0.0).astype(BF16)
            in_side = jnp.dot(ins[at].reshape(64, 128), spread, preferred_element_type=F32)
            rows = pl.ds(pl.multiple_of(skip * PAIR + n * 64, 64), 64)
            sign[rows, :] = (in_side * sign[rows, :].astype(F32)).astype(BF16)

    for cp in factor_loads:
        cp.wait()
    factor(0, GROUP)

    def take(q, one):
        @pl.when(q >= skip)
        def _():
            arrive(q, one)
            assemble(q, one)

    def pass_on(q, parity):
        pl.when((q >= skip) & (q < total))(lambda: turn(q, parity))
        if pairs > PRE and parity == skip:

            @pl.when(q == skip)
            def _():
                for i in range(4):
                    ahead(i, 0).wait_recv()
                for i in range(4):
                    ahead(i, 1).start()

            @pl.when(q + LOOK == early)
            def _():
                for i in range(4):
                    ahead(i, 1).wait_recv()

        pl.when((q >= skip) & (q + LOOK < total))(lambda: send(q + LOOK))

    @pl.loop(0, groups + 1)
    def _(n):
        pl.when(n >= 1)(lambda: take((n - 1) * GROUP, 0))
        pass_on(n * GROUP, 0)
        pl.when(n >= 1)(lambda: take((n - 1) * GROUP + 1, 1))

        @pl.loop(0, 2)
        def _(i):
            pl.when(n >= 1)(lambda: multiply(n - 1, GROUP, i))

            @pl.when(i == 0)
            def _():
                if skip:
                    pass_on(n * GROUP + 1, 1)
                pl.when(n == 0)(lambda: factor(1, GROUP))
                if not skip:
                    pass_on(n * GROUP + 1, 1)

        pl.when(n >= 1)(lambda: project(n - 1, GROUP))

        @pl.when(n == 0)
        def _():
            for cp in gathers:
                cp.wait_recv()
            for cp in last_loads:
                cp.wait()
            sign_sides()

        pl.when(n + 2 < groups)(lambda: factor(n + 2, GROUP))

    mine = jnp.concatenate([diff[...].T, jnp.broadcast_to(gap[0:1, 0:1], (128, 64))], 1).reshape(TENSOR, 8, 128)
    upper = (iota((TENSOR, 8, 128), 2) >= 64) & (iota((TENSOR, 8, 128), 1) >= 4)
    outs[...] = jnp.where(upper, gap[4:5, 0:1].reshape(1, 1, 1), mine)
    reduces = []
    for d in FAR:
        to = lax.rem(t + d, TENSOR)
        cp = remote(outs.at[to], sides.at[t], rsend.at[d - 1], rrecv.at[d - 1], g, to)
        cp.start()
        reduces.append(cp)
    sides[t] = outs[t]
    @pl.loop(skip, total)
    def _(q):
        for i in range(4):
            second(q, i, 0).wait_send()

    for q in range(skip, total):
        for i in range(4):
            second(q, i, 1, q % 2).wait_send()

    if pairs > PRE:
        for hop in range(2):
            for i in range(4):
                ahead(i, hop).wait_send()
    for cp in gathers:
        cp.wait_send()
    for cp in reduces:
        cp.wait_recv()
    summed = jnp.sum(sides[...], axis=0)
    coeff = -BETA * jax.nn.sigmoid(-BETA * summed[:, 64:65])
    scaled = coeff * summed
    even, odd = (jnp.concatenate([scaled[i + e : i + e + 1] for i in (0, 2, 4, 6)], 0) for e in (0, 1))
    fin[...] = jnp.where(iota((4, 128), 1) < 64, even, pltpu.roll(odd, 64, 1))

    ends = []
    own_column = remote(fin, coled.at[g, column_part], csend.at[0], crecv.at[g, column_part], column_group, t)
    for d in FAR:
        ends.append(remote(fin, coled.at[g, column_part], csend.at[d], crecv.at[g, column_part], column_group, lax.rem(t + d, TENSOR)))
    for d in FAR:
        ends.append(remote(fin, every.at[t], gsend.at[d - 1], grecv.at[d - 1], g, lax.rem(t + d, TENSOR)))
    for d in range(1, GROUPS):
        ends.append(remote(fin, rowed.at[g], psend.at[d - 1], precv.at[d - 1], lax.rem(g + d, GROUPS), t))
    for cp in ends:
        cp.start()
    pl.when(column_group != g)(own_column.start)

    @pl.when(column_group == g)
    def _():
        coled[g, column_part] = fin[...]

    rowed[g] = fin[...]
    every[t] = fin[...]
    for cp in reduces:
        cp.wait_send()

    for cp in ends[-(GROUPS - 1) :]:
        cp.wait_recv()
    for d in range(GROUPS):
        for h in range(2):
            of = lax.rem(g + d, GROUPS)
            cp = remote(fin, coled.at[of, h], csend.at[0], crecv.at[of, h], column_group, t)
            if d == 0:
                pl.when(2 * g + h != t)(cp.wait_recv)
            else:
                cp.wait_recv()

    for cp in ends[TENSOR - 1 : 2 * TENSOR - 2]:
        cp.wait_recv()
    ends_o[0:8] = rowed[...]
    ends_o[8:24] = coled[...].reshape(TENSOR, 4, 128)
    ends_o[24:40] = every[...]

    pl.when(column_group != g)(own_column.wait_send)
    for cp in ends:
        cp.wait_send()


def main(pairs, gap, insum, sign, pout, own, g1, pick, gate, upo, w):
    total = pairs + pairs % GROUP
    vmem = pl.BlockSpec(memory_space=pltpu.VMEM)
    hbm = pl.BlockSpec(memory_space=pl.ANY)
    dma = pltpu.SemaphoreType.DMA
    return pl.pallas_call(
        functools.partial(main_kernel, pairs),
        out_shape=jax.ShapeDtypeStruct((40, 4, 128), F32),
        in_specs=[vmem] + [hbm] * 9,
        out_specs=vmem,
        scratch_shapes=[
            pltpu.VMEM((2, total, 4, 4, ROWS, 128), BF16),
            pltpu.VMEM((HIDDEN, MODEL), BF16),
            pltpu.VMEM((HIDDEN, TOKENS), BF16),
            pltpu.VMEM((HIDDEN, TOKENS), BF16),
            pltpu.VMEM((total * PAIR, TOKENS), BF16),
            pltpu.VMEM((total * PAIR, 128), BF16),
            pltpu.VMEM((RANK, HIDDEN), BF16),
            pltpu.VMEM((HIDDEN, total * PAIR), F32),
            pltpu.VMEM((GROUP * PAIR, MODEL), BF16),
            pltpu.VMEM((HIDDEN, GROUP * PAIR), BF16),
            pltpu.VMEM((TENSOR, 8, 128), F32),
            pltpu.VMEM((RANK, 128), F32),
            pltpu.VMEM((TENSOR, 8, 128), F32),
            pltpu.VMEM((TENSOR, 32, 128), BF16),
            pltpu.VMEM((4, 128), F32),
            pltpu.VMEM((TENSOR, 4, 128), F32),
            pltpu.VMEM((GROUPS, 4, 128), F32),
            pltpu.VMEM((GROUPS, 2, 4, 128), F32),
            dma((14,)),
            dma((TENSOR - 1,)),
            dma((TENSOR - 1,)),
            dma((8,)),
            dma((8,)),
            dma((total, 8)),
            dma((total, 8)),
            dma((TENSOR - 1,)),
            dma((TENSOR - 1,)),
            dma((TENSOR - 1,)),
            dma((TENSOR - 1,)),
            dma((GROUPS - 1,)),
            dma((GROUPS - 1,)),
            dma((TENSOR,)),
            dma((GROUPS, 2)),
        ],
        compiler_params=pltpu.CompilerParams(collective_id=pairs, has_side_effects=True, vmem_limit_bytes=60 << 20),
        cost_estimate=pl.CostEstimate(flops=25_000_000 * PAIR * pairs, bytes_accessed=30_000_000, transcendentals=8),
        name=f"gather_{pairs}",
    )(gap, insum, sign, pout, own, g1, pick, gate, upo, w)


def final_kernel(ends, grads_o, fisher_o):
    def joined(at, h):
        return jnp.concatenate([ends[at, h], ends[at, 2 + h]], 0)

    right = jnp.concatenate([joined(pl.ds(8 + part, GROUPS, 2), h) for part in range(2) for h in range(2)], 1)
    left = jnp.concatenate([joined(slice(0, GROUPS), h) for h in range(2)], 1)
    fisher_o[...] = lax.dot_general(left, right, TN, precision=lax.Precision.HIGHEST, preferred_element_type=F32)
    for c in range(TENSOR):
        tile = ends[24 + c]
        for h in range(2):
            at = c * 256 + h * 128
            grads_o[:, at : at + 128] = jnp.concatenate([tile[h : h + 1], tile[2 + h : 3 + h]], 0)


def final(ends):
    sds = jax.ShapeDtypeStruct
    vmem = pl.BlockSpec(memory_space=pltpu.VMEM)
    return pl.pallas_call(
        final_kernel,
        out_shape=(sds((2, RANK * RANK), F32), sds((256, 512), F32)),
        in_specs=[vmem],
        out_specs=(vmem, vmem),
        cost_estimate=pl.CostEstimate(flops=4_000_000, bytes_accessed=700_000, transcendentals=0),
        name="final",
    )(ends)


def per_device(
    activations, upstream, gate_pre, up_out, w_down, proj_in, proj_out, policy_logp, ref_logp, loss_mask, resp_len, pair_perm, chosen_first
):
    own, g1, pick, sign, insum, count, gap = stage(
        pair_perm, chosen_first, resp_len, loss_mask, policy_logp, ref_logp, upstream.T, activations.T, proj_in
    )
    args = (gap, insum, sign, proj_out, own, g1, pick, gate_pre.T, up_out.T, w_down)
    if len(SIZES) == 1:
        return final(main(SIZES[0], *args))
    return final(lax.switch(count[0], [functools.partial(main, size) for size in SIZES], *args))


def solution(mesh):
    placed = (
        P("dp", "tensor"),
        P("dp", "tensor"),
        P("dp", "tensor"),
        P("dp", "tensor"),
        P("tensor", None),
        P(None, "tensor"),
        P(None, "tensor"),
        P("dp", "tensor"),
        P("dp", "tensor"),
        P("dp", None),
        P("dp"),
        P("dp", None),
        P("dp"),
    )
    return jax.shard_map(
        per_device,
        mesh=mesh,
        in_specs=placed,
        out_specs=(P("dp", None), P("tensor", "dp")),
        check_vma=False,
    )
```
